256 devices in a mesh: dp: 32 (over y, z), tensor: 8 (over x, core).
Axes of the slice: x: 4, y: 4, z: 8, core: 2. Of those that a mesh axis runs over, the one named last changes fastest.
Arguments:
- hidden: bfloat16 [512, 256, 768], P(('dp', 'tensor')), may hold values from -64 to 64
- lengths: int32 [512], P('dp'), may hold values from 64 to 256, as said below
- owner_of: int32 [512, 1], P('dp'), may hold values from 0 to 31; in each aligned block of 16 rows (0 to 15, 16 to 31, ...) at most 2 rows name the same one
- list_local: int32 [512], P('dp'), may hold values from 0 to 1023
- old_weight: int32 [32768], P('dp'), may hold values from 1 to 8
- old_centroids: float32 [32768, 768], P('dp'), may hold values from -6 to 6
- w_qkv: bfloat16 [768, 2304], P('dp'), may hold values from -0.21875 to 0.21875
- w_out: bfloat16 [768, 768], P('dp'), may hold values from -0.21875 to 0.21875
- gain_one: float32 [768], replicated, may hold values from 0.1 to 1.9
- shift_one: float32 [768], replicated, may hold values from -2 to 2
- w_up: bfloat16 [768, 3072], P('dp', 'tensor'), may hold values from -0.21875 to 0.21875
- w_down: bfloat16 [3072, 768], P('tensor', 'dp'), may hold values from -0.109375 to 0.109375
- gain_two: float32 [768], replicated, may hold values from 0.1 to 1.9
- shift_two: float32 [768], replicated, may hold values from -2 to 2
- rotation: float32 [768, 768], P('tensor'), may hold values from -0.21875 to 0.21875
Outputs:
- rotated: float32 [512, 768], P('dp', 'tensor')
- centroids: float32 [32768, 768], P('dp')
The draws below stay inside these ranges and needn't reach their ends.
Inputs may be any that keep to these rules, and one draw needn't show every extreme that they name: `lengths`: some passage has 256 tokens in every draw. `owner_of`: among the passages of one index of dp, at most 2 name the same owner.
All inputs are finite; a program needn't handle non-finite values.
Results may differ from the reference program's by a relative error of at most 0.003.
Values may be sent and summed in bfloat16 or wider, within the bound.
A program may use at most 64 MiB of HBM per device.

```python
import math
import jax
import jax.numpy as jnp
import numpy as np
from jax import lax

D = 768
HEADS = 12
HEAD_DIM = 64
FF = 3072
L = 256
LISTS_DEV = 1024
P_GRP = 16
PASSAGES = 512
CAP = 2
LISTS = 32768
FT = 384
N_DP = 32
N_TENSOR = 8


def draw_hidden(key, part):
    key_common = jax.random.fold_in(key, 11)
    key_own = jax.random.fold_in(key, 12)
    common = jnp.clip(jax.random.normal(key_common, (PASSAGES, 1, D), jnp.float32), -3.0, 3.0)
    own = jnp.clip(jax.random.normal(key_own, (PASSAGES, L, D), jnp.float32), -3.0, 3.0)
    return (common + own).astype(jnp.bfloat16)


def draw_lengths(key, part):
    drawn = jax.random.randint(jax.random.fold_in(key, 21), (PASSAGES,), L // 4, L + 1)
    return drawn.at[::P_GRP].set(L).astype(jnp.int32)


def plant(values, rng, least, high):
    index_at = [jax.random.randint(jax.random.fold_in(rng, axis), (), 0, length) for axis, length in enumerate(values.shape)]
    longest = values.shape.index(max(values.shape))
    next_to = index_at[:longest] + [(index_at[longest] + 1) % values.shape[longest]] + index_at[longest + 1:]
    return values.at[tuple(index_at)].set(least).at[tuple(next_to)].set(high)


def shard_levels(stream_key, extent, shards, least, largest):
    def one(position, shards_of):
        steps = jax.random.uniform(jax.random.fold_in(jax.random.fold_in(stream_key, 6), position), (shards_of,), jnp.float32, least / len(shards), largest / len(shards))
        return jnp.repeat(jnp.exp(steps), extent[position] // shards_of).reshape((-1,) + (1,) * (len(extent) - position - 1))

    loudness = one(*shards[0])
    for cut in shards[1:]:
        loudness = loudness * one(*cut)
    return loudness


def routed_block(rng, own, number, rows, amount, top, bound, slope):
    sequence = jax.random.permutation(rng, amount)
    heavy_load, usual = portions_of(amount, rows * top, bound, slope, True), portions_of(amount, rows * top, bound, slope, False)
    places = jnp.arange(amount)

    def named(tallies, turn):
        used = int((tallies > 0).sum())
        fixed = max(1, used // 4)
        moved = fixed + (places - fixed + turn * (used - fixed)) % max(1, amount - fixed)
        return jnp.zeros((amount,), jnp.int32).at[sequence[jnp.where(places < fixed, places, moved)]].set(jnp.asarray(tallies, jnp.int32))

    tallies = jnp.where(number % 4 == 0, named(heavy_load, number // 4), named(usual, number - number // 4 - 1))
    mixed = jax.random.permutation(jax.random.fold_in(own, 3), amount)
    source_of, taker = mixed[0:amount // 2 * 2:2], mixed[1:amount // 2 * 2:2]
    margin = jnp.minimum(tallies[source_of] - 1, bound - tallies[taker]) // 2
    margin = jnp.where((source_of == sequence[0]) | (taker == sequence[0]) | (tallies[taker] == 0), 0, jnp.maximum(margin, 0))
    moved = jax.random.randint(jax.random.fold_in(own, 4), (amount // 2,), 0, 1 << 20) % (margin + 1)
    tallies = tallies.at[source_of].add(-moved).at[taker].add(moved)
    items = jnp.searchsorted(jnp.cumsum(tallies), jnp.arange(rows * top), side="right").astype(jnp.int32)
    table = items.reshape(top, rows).T
    table = table[jax.random.permutation(jax.random.fold_in(own, 1), rows)]
    turn = jax.random.randint(jax.random.fold_in(own, 2), (rows, 1), 0, top)
    return jnp.take_along_axis(table, (jnp.arange(top)[None, :] + turn) % top, axis=1)


def portions_of(number_of, total, limit, lean, full):
    weights = [(1 << 20) // math.isqrt(rank ** lean) + 1 for rank in range(1, number_of + 1)]
    largest = limit if full else min(limit, max(-(-total // number_of), total * weights[0] // sum(weights)))
    least = 1 if total - largest >= number_of - 1 else 0
    holding, rest = [largest] + [least] * (number_of - 1), total - largest - least * (number_of - 1)
    while rest > 0:
        movable = [i for i in range(1, number_of) if holding[i] < largest] or [i for i in range(1, number_of) if holding[i] < limit]
        mass, remaining = sum([weights[i] for i in movable]), rest
        for i in movable:
            addition = min(limit - holding[i], max(1, remaining * weights[i] // mass), rest)
            holding[i] = holding[i] + addition
            rest = rest - addition
    return np.array(holding)


def bell_draw(rng, dims, scale, most, shards=(), kind=jnp.bfloat16):
    values = scale * jax.random.normal(rng, dims, jnp.float32)
    if shards:
        values = values * shard_levels(rng, dims, shards, -0.22, 0.18)
    return jnp.clip(values, -most, most).astype(kind)


def setup_inputs(seed: int = 0) -> dict:
    splits = jax.random.split(jax.random.key(seed), 16)
    hidden = draw_hidden(jax.random.fold_in(splits[15], 71), 0)
    lengths = draw_lengths(jax.random.fold_in(splits[15], 71), 0)
    owner_of_keys = jax.random.split(jax.random.fold_in(splits[2], 1), PASSAGES // P_GRP)
    owner_of_turns = jax.random.permutation(jax.random.fold_in(splits[2], 3), PASSAGES // P_GRP)
    owner_of = jax.vmap(lambda own, number: routed_block(jax.random.fold_in(splits[2], 2), own, number, P_GRP, N_DP, 1, CAP, 2))(owner_of_keys, owner_of_turns).reshape((PASSAGES, 1))
    list_local = plant(jax.random.randint(splits[3], (PASSAGES,), 0, LISTS_DEV), jax.random.fold_in(splits[3], 1), 0, LISTS_DEV - 1).astype(jnp.int32)
    old_weight = plant(jax.random.randint(splits[4], (LISTS,), 1, 9), jax.random.fold_in(splits[4], 1), 1, 8).astype(jnp.int32)
    old_centroids = bell_draw(splits[5], (LISTS, D), 1.0, 6.0, ((0, 32),), jnp.float32)
    w_qkv = bell_draw(splits[6], (D, 3 * D), D ** -0.5, 0.21875, ((0, 32),))
    w_out = bell_draw(splits[7], (D, D), D ** -0.5, 0.21875, ((0, 32),))
    gain_one = jnp.clip(1.0 + 0.18 * jax.random.normal(splits[8], (D,), jnp.float32), 0.1, 1.9)
    shift_one = bell_draw(splits[9], (D,), 0.4, 2.0, (), jnp.float32)
    w_up = bell_draw(splits[10], (D, FF), D ** -0.5, 0.21875, ((0, 32), (1, 8)))
    w_down = bell_draw(splits[11], (FF, D), FF ** -0.5, 0.109375, ((0, 8), (1, 32)))
    gain_two = jnp.clip(1.0 + 0.18 * jax.random.normal(splits[12], (D,), jnp.float32), 0.1, 1.9)
    shift_two = bell_draw(splits[13], (D,), 0.4, 2.0, (), jnp.float32)
    rotation = bell_draw(splits[14], (D, D), D ** -0.5, 0.21875, ((0, 8),), jnp.float32)
    return dict(hidden=hidden, lengths=lengths, owner_of=owner_of, list_local=list_local, old_weight=old_weight, old_centroids=old_centroids, w_qkv=w_qkv, w_out=w_out, gain_one=gain_one, shift_one=shift_one, w_up=w_up, w_down=w_down, gain_two=gain_two, shift_two=shift_two, rotation=rotation)


EPS = 1e-05

def norm_rows(values, gain, shift):
    mean = lax.optimization_barrier(jnp.mean(values, axis=-1, keepdims=True))
    centered = values - mean
    spread = lax.optimization_barrier(jnp.mean(centered * centered, axis=-1, keepdims=True))
    return centered * lax.rsqrt(spread + EPS) * gain + shift

def encode(states, lens, w_qkv, w_out, gain_one, shift_one, w_up, w_down, gain_two, shift_two):
    count = states.shape[0]
    flat = states.reshape(count * L, D)
    qkv = jnp.dot(flat, w_qkv, preferred_element_type=jnp.float32).astype(jnp.bfloat16)
    qkv = qkv.reshape(count, L, 3, HEADS, HEAD_DIM).astype(jnp.float32)
    scores = jnp.einsum('plhe,pmhe->phlm', qkv[:, :, 0], qkv[:, :, 1]) * HEAD_DIM ** (-0.5)
    keys_ok = jnp.arange(L)[None, None, None, :] < lens[:, None, None, None]
    scores = jnp.where(keys_ok, scores, -1e+30)
    probs = jax.nn.softmax(scores, axis=-1).astype(jnp.bfloat16).astype(jnp.float32)
    context = jnp.einsum('phlm,pmhe->plhe', probs, qkv[:, :, 2]).astype(jnp.bfloat16)
    context = context.reshape(count * L, D)
    mixed = jnp.dot(context, w_out, preferred_element_type=jnp.float32)
    first = norm_rows(flat.astype(jnp.float32) + mixed, gain_one, shift_one).astype(jnp.bfloat16)
    act = jax.nn.gelu(jnp.dot(first, w_up, preferred_element_type=jnp.float32), approximate=False).astype(jnp.bfloat16)
    total = jnp.zeros((count * L, D), jnp.float32)
    for piece in range(N_TENSOR):
        part = jnp.dot(act[:, piece * FT:(piece + 1) * FT], w_down[piece * FT:(piece + 1) * FT], preferred_element_type=jnp.float32)
        if piece == 0:
            part = part + first.astype(jnp.float32)
        part = lax.optimization_barrier(part.astype(jnp.bfloat16)).astype(jnp.float32)
        total = total + part
    second = norm_rows(total, gain_two, shift_two).reshape(count, L, D)
    tok_ok = jnp.arange(L)[None, :] < lens[:, None]
    pooled = lax.optimization_barrier(jnp.sum(jnp.where(tok_ok[:, :, None], second, 0.0), axis=1)) / lens[:, None].astype(jnp.float32)
    return pooled

def reference(hidden, lengths, owner_of, list_local, old_weight, old_centroids, w_qkv, w_out, gain_one, shift_one, w_up, w_down, gain_two, shift_two, rotation):
    grouped = hidden.reshape(N_DP, P_GRP, L, D)
    grouped_lens = lengths.reshape(N_DP, P_GRP)

    def one_group(items):
        return encode(items[0], items[1], w_qkv, w_out, gain_one, shift_one, w_up, w_down, gain_two, shift_two)
    emb = lax.map(one_group, (grouped, grouped_lens)).reshape(PASSAGES, D)
    lists = (owner_of[:, 0] * LISTS_DEV + list_local).astype(jnp.int32)
    sums = jax.ops.segment_sum(emb, lists, num_segments=LISTS)
    counts = jax.ops.segment_sum(jnp.ones((PASSAGES,), emb.dtype), lists, num_segments=LISTS)
    weight = old_weight.astype(emb.dtype)
    centroids = (weight[:, None] * old_centroids + sums) / (weight + counts)[:, None]
    resid = emb - centroids[lists]
    rotated = jnp.dot(resid, rotation, precision=lax.Precision.HIGHEST)
    return (rotated, centroids)
```

```python
import jax
import jax.numpy as jnp
from jax import lax
from jax.sharding import PartitionSpec as P

HEADS = 12
HEAD_DIM = 64


EPS = 1e-05


def norm_rows(values, gain, shift):
    mean = jnp.mean(values, axis=-1, keepdims=True)
    centered = values - mean
    spread = jnp.mean(centered * centered, axis=-1, keepdims=True)
    return centered * lax.rsqrt(spread + EPS) * gain + shift


def pool_valid(states, lens):
    width = states.shape[1]
    tok_ok = jnp.arange(width)[None, :] < lens[:, None]
    summed = jnp.sum(jnp.where(tok_ok[:, :, None], states, 0.0), axis=1)
    return summed / lens[:, None].astype(jnp.float32)


def local(
    hidden,
    lengths,
    owner_of,
    list_local,
    old_weight,
    old_centroids,
    w_qkv,
    w_out,
    gain_one,
    shift_one,
    w_up,
    w_down,
    gain_two,
    shift_two,
    rotation,
):
    count, slots_len, width = hidden.shape
    rows = count * slots_len
    tens = lax.axis_index("tensor")
    my_lens = lax.dynamic_slice_in_dim(lengths, tens * count, count)
    flat = hidden.reshape(rows, width)
    cols = flat
    qkv = jnp.dot(
        cols, lax.all_gather(w_qkv, "dp", axis=0, tiled=True), preferred_element_type=jnp.float32
    )
    qkv = qkv.astype(jnp.bfloat16).reshape(count, slots_len, 3, HEADS, HEAD_DIM)
    scores = jnp.einsum(
        "plhe,pmhe->phlm", qkv[:, :, 0], qkv[:, :, 1], preferred_element_type=jnp.float32
    ) * HEAD_DIM ** (-0.5)
    keys_ok = jnp.arange(slots_len)[None, None, None, :] < my_lens[:, None, None, None]
    scores = jnp.where(keys_ok, scores, -1e30)
    probs = jax.nn.softmax(scores, axis=-1).astype(jnp.bfloat16)
    context = jnp.einsum("phlm,pmhe->plhe", probs, qkv[:, :, 2], preferred_element_type=jnp.float32)
    context = context.astype(jnp.bfloat16).reshape(rows, width)
    cols = context
    mixed = jnp.dot(
        cols, lax.all_gather(w_out, "dp", axis=0, tiled=True), preferred_element_type=jnp.float32
    )
    first = norm_rows(flat.astype(jnp.float32) + mixed, gain_one, shift_one).astype(jnp.bfloat16)
    up_full, down_full = (
        lax.all_gather(w_up, "dp", axis=0, tiled=True),
        lax.all_gather(w_down, "dp", axis=1, tiled=True),
    )
    n_tens = lax.axis_size("tensor")
    group = count * n_tens
    feat = width // n_tens
    leader = (tens == 0).astype(jnp.float32)
    piece = lax.all_gather(first, "tensor", axis=0, tiled=True)
    act = jax.nn.gelu(
        jnp.dot(piece, up_full, preferred_element_type=jnp.float32), approximate=False
    ).astype(jnp.bfloat16)
    terms = jnp.dot(act, down_full, preferred_element_type=jnp.float32) + leader * piece.astype(
        jnp.float32
    )
    total = lax.psum_scatter(
        terms.astype(jnp.bfloat16), "tensor", scatter_dimension=0, tiled=True
    ).astype(jnp.float32)
    second = norm_rows(total, gain_two, shift_two).reshape(count, slots_len, width)
    pooled = pool_valid(second, my_lens)
    emb = lax.all_to_all(pooled, "tensor", split_axis=1, concat_axis=0, tiled=True)
    n_owners = lax.axis_size("dp")
    capacity = max(2, 2 * group // n_owners)
    slot_total = n_owners * capacity
    owner = owner_of[:, 0]
    places = jnp.arange(group)
    earlier = (owner[:, None] == owner[None, :]) & (places[None, :] < places[:, None])
    rank = jnp.sum(earlier.astype(jnp.int32), axis=1)
    slot = owner * capacity + rank
    placed = slot[None, :] == jnp.arange(slot_total)[:, None]
    send_emb = jnp.dot(placed.astype(jnp.float32), emb, precision=lax.Precision.HIGHEST)
    send_list = jnp.max(jnp.where(placed, list_local[None, :], -1), axis=1)
    recv_emb, recv_list = (
        lax.all_to_all(send_emb, "dp", split_axis=0, concat_axis=0, tiled=True),
        lax.all_to_all(send_list, "dp", split_axis=0, concat_axis=0, tiled=True),
    )
    recv_vals = lax.all_gather(recv_emb, "tensor", axis=1, tiled=True)
    owned = old_weight.shape[0]
    list_hot = (recv_list[:, None] == jnp.arange(owned)[None, :]).astype(jnp.float32)
    sums = lax.dot_general(
        list_hot, recv_vals, (((0,), (0,)), ((), ())), precision=lax.Precision.HIGHEST
    )
    counts = jnp.sum(list_hot, axis=0)
    weight = old_weight.astype(jnp.float32)
    centroids = (weight[:, None] * old_centroids + sums) / (weight + counts)[:, None]
    resid = recv_vals - jnp.dot(list_hot, centroids, precision=lax.Precision.HIGHEST)
    resid_part = lax.dynamic_slice_in_dim(resid, tens * feat, feat, 1)
    returned = lax.all_to_all(resid_part, "dp", split_axis=0, concat_axis=0, tiled=True)
    mine = lax.dot_general(
        placed.astype(jnp.float32),
        returned,
        (((0,), (0,)), ((), ())),
        precision=lax.Precision.HIGHEST,
    )
    partial_rot = jnp.dot(mine, rotation, precision=lax.Precision.HIGHEST)
    rotated = lax.psum_scatter(partial_rot, "tensor", scatter_dimension=1, tiled=True)
    return (rotated, centroids)


def solution(mesh):
    return jax.shard_map(
        local,
        mesh=mesh,
        in_specs=(
            P(("dp", "tensor"), None, None),
            P("dp"),
            P("dp", None),
            P("dp"),
            P("dp"),
            P("dp", None),
            P("dp", None),
            P("dp", None),
            P(),
            P(),
            P("dp", "tensor"),
            P("tensor", "dp"),
            P(),
            P(),
            P("tensor", None),
        ),
        out_specs=(P("dp", "tensor"), P("dp", None)),
        check_vma=False,
    )
```

```python
import functools

import jax
import jax.numpy as jnp
from jax import lax
from jax.experimental import pallas as pl
from jax.experimental.pallas import tpu as pltpu
from jax.sharding import PartitionSpec as P

EPS = 1e-05
MESH = pl.DeviceIdType.MESH
F32 = jnp.float32
BF16 = jnp.bfloat16

L = 256
D = 768
SLAB = 384
N_Y = 4
N_Z = 8
N_X = 4
ROWS = 512


def split3(values):
    high = values.astype(BF16)
    rest = values - high.astype(F32)
    mid = rest.astype(BF16)
    low = (rest - mid.astype(F32)).astype(BF16)
    return high, mid, low


def pick(hot, values):
    parts = split3(values)
    return sum(jnp.dot(hot, part, preferred_element_type=F32) for part in parts)


class Ring:
    def __init__(self, sems, n, me, right, left, block, halves):
        self.n, self.me, self.right, self.left = n, me, right, left
        self.block, self.halves = block, halves
        self.sems = sems
        self.ids = [(sems.take(), sems.take()) for _ in range(n // 2)]

    def _at(self, offset):
        return lax.rem(self.me + offset + self.n, self.n)

    def _refs(self, step):
        last = step == self.n // 2
        out_right, out_left = self._at(-(step - 1)), self._at(step - 1)
        in_left, in_right = self._at(-step), self._at(step)
        if last:
            return (
                self.halves(out_right)[0],
                self.halves(out_left)[1],
                self.halves(in_left)[0],
                self.halves(in_right)[1],
            )
        return tuple(self.block(i) for i in (out_right, out_left, in_left, in_right))

    def start(self, step):
        to_right, to_left, _, _ = self._refs(step)
        a, b = self.ids[step - 1]
        self.sems.send(to_right, a, self.right)
        self.sems.send(to_left, b, self.left)

    def wait(self, step):
        _, _, from_left, from_right = self._refs(step)
        a, b = self.ids[step - 1]
        self.sems.arrived(from_left, a, self.right)
        self.sems.arrived(from_right, b, self.left)


class Copies:
    def __init__(self, send, recv):
        self.send_sems, self.recv_sems = send, recv
        self.count = 0
        self.started = []

    def take(self):
        self.count += 1
        return self.count - 1

    def _copy(self, src, dst, number, device):
        return pltpu.make_async_remote_copy(
            src_ref=src,
            dst_ref=dst,
            send_sem=self.send_sems.at[number],
            recv_sem=self.recv_sems.at[number],
            device_id=device,
            device_id_type=MESH,
        )

    def send(self, src, number, device, dst=None):
        copy = self._copy(src, src if dst is None else dst, number, device)
        copy.start()
        self.started.append(copy)

    def arrived(self, ref, number, device):
        self._copy(ref, ref, number, device).wait_recv()

    def finish(self):
        for copy in self.started:
            copy.wait_send()


N_COPIES = 160


def encode_kernel(
    x_ref,
    lens_ref,
    ids_ref,
    weight_ref,
    old_ref,
    wqkv_ref,
    wout_ref,
    gain_one_ref,
    shift_one_ref,
    wup_ref,
    wdown_ref,
    gain_two_ref,
    shift_two_ref,
    rot_ref,
    emb_out,
    ids_out,
    rows_out,
    rot_out,
    w_a,
    w_u,
    w_d,
    z_a,
    z_u,
    z_d,
    turned,
    old_buf,
    rot_send,
    mine_rows,
    owner_rows,
    emb_group,
    qkv,
    ctx,
    first,
    acc,
    send_sems,
    recv_sems,
    local_sems,
):
    dp = lax.axis_index("dp")
    tens = lax.axis_index("tensor")
    y, z = dp // N_Z, lax.rem(dp, N_Z)
    x, core = tens // 2, lax.rem(tens, 2)

    def at_y(i):
        return (i * N_Z + z, tens)

    def at_z(i):
        return (y * N_Z + i, tens)

    y_right, y_left = at_y(lax.rem(y + 1, N_Y)), at_y(lax.rem(y + N_Y - 1, N_Y))
    z_right, z_left = at_z(lax.rem(z + 1, N_Z)), at_z(lax.rem(z + N_Z - 1, N_Z))
    peers = [(dp, lax.rem(tens + k, 8)) for k in range(1, 8)]
    sibling = (dp, 2 * x + 1 - core)
    is_turn_self = tens == z
    turn = [(i * N_Z + tens, z) for i in range(N_Y)]

    old_copy = pltpu.make_async_copy(old_ref, old_buf, local_sems.at[0])
    old_copy.start()

    barrier = pltpu.get_barrier_semaphore()
    for device in [y_right, y_left, z_right, z_left] + peers:
        pl.semaphore_signal(barrier, inc=1, device_id=device, device_id_type=MESH)
    for i in range(N_Y):
        @pl.when(jnp.logical_not(jnp.logical_and(is_turn_self, y == i)))
        def _():
            pl.semaphore_signal(barrier, inc=1, device_id=turn[i], device_id_type=MESH)

    for s in range(3):
        z_a[z, s] = wqkv_ref[:, pl.ds(pl.multiple_of((2 * s + core) * SLAB, 128), SLAB)]
    z_a[z, 3] = wout_ref[:, pl.ds(pl.multiple_of(core * SLAB, 128), SLAB)]
    z_u[z, x] = wup_ref[...]
    z_d[z, x] = wdown_ref[...]
    ids_out[y, z] = ids_ref[...]
    for k in range(8):
        rot_send[k] = rot_ref[:, k * 96 : (k + 1) * 96]

    pl.semaphore_wait(barrier, 11 + N_Y - is_turn_self.astype(jnp.int32))

    sems = Copies(send_sems, recv_sems)

    def z_ring(buf):
        return Ring(
            sems, N_Z, z, z_right, z_left,
            lambda i: buf.at[i],
            lambda i: (buf.at[i, pl.ds(0, 2)], buf.at[i, pl.ds(2, 2)]),
        )

    def rows_of(i):
        return pl.ds(pl.multiple_of(i * 192, 64), 192)

    def y_ring(buf):
        return Ring(
            sems, N_Y, y, y_right, y_left,
            lambda i: buf.at[pl.ds(core * 4, 4), rows_of(i)],
            lambda i: (
                buf.at[pl.ds(core * 4, 2), rows_of(i)],
                buf.at[pl.ds(core * 4 + 2, 2), rows_of(i)],
            ),
        )

    za, zu, zd = z_ring(z_a), z_ring(z_u), z_ring(z_d)
    ya, yu, yd = y_ring(w_a), y_ring(w_u), y_ring(w_d)
    zi = Ring(
        sems, N_Z, z, z_right, z_left,
        lambda i: ids_out.at[y, i],
        lambda i: (ids_out.at[y, i, pl.ds(0, 8)], ids_out.at[y, i, pl.ds(8, 8)]),
    )
    yi = Ring(
        sems, N_Y, y, y_right, y_left,
        lambda i: ids_out.at[i],
        lambda i: (ids_out.at[i, pl.ds(0, 4)], ids_out.at[i, pl.ds(4, 4)]),
    )

    def same_chip(buf):
        numbers = [sems.take() for _ in range(N_Y)]

        def send(offset):
            i = lax.rem(y + offset + N_Y, N_Y)
            sems.send(buf.at[pl.ds(core * 4, 4), rows_of(i)], numbers[offset], sibling)

        def wait(offset):
            i = lax.rem(y + offset + N_Y, N_Y)
            sems.arrived(
                buf.at[pl.ds((1 - core) * 4, 4), rows_of(i)], numbers[offset], sibling
            )

        return send, wait

    sa, su, sd = same_chip(w_a), same_chip(w_u), same_chip(w_d)

    def assemble(buf, full):
        for s in range(4):
            for i in range(N_Z):
                turned[i * 24 : (i + 1) * 24, :] = buf[i, s].astype(F32)
            full[core * 4 + s, rows_of(y), :] = turned[...].astype(BF16)

    za.start(1)
    zi.start(1)
    x_numbers = [(sems.take(), sems.take()) for _ in range(3)]
    for k in range(1, 4):
        device = (dp, lax.rem(tens + 2 * k, 8))
        sems.send(z_u.at[z, x], x_numbers[k - 1][0], device)
        sems.send(z_d.at[z, x], x_numbers[k - 1][1], device)
    rot_numbers = [sems.take() for _ in range(7)]
    rot_place = pl.ds(pl.multiple_of(tens * 96, 32), 96)
    rot_out[rot_place, :] = rot_send[tens]
    for k in range(1, 8):
        other = lax.rem(tens + k, 8)
        sems.send(
            rot_send.at[other], rot_numbers[k - 1], peers[k - 1], dst=rot_out.at[rot_place]
        )
    for step in (2, 3, 4):
        za.wait(step - 1)
        za.start(step)
        zi.wait(step - 1)
        zi.start(step)
    za.wait(4)
    zi.wait(4)
    assemble(z_a, w_a)
    ya.start(1)
    yi.start(1)
    sa[0](0)
    for k in range(1, 4):
        origin = lax.rem(x + N_X - k, N_X)
        device = (dp, lax.rem(tens + 2 * k, 8))
        sems.arrived(z_u.at[z, origin], x_numbers[k - 1][0], device)
        sems.arrived(z_d.at[z, origin], x_numbers[k - 1][1], device)
    zu.start(1)
    zd.start(1)
    ya.wait(1)
    ya.start(2)
    yi.wait(1)
    yi.start(2)
    sa[0](1)
    sa[0](3)
    for step in (2, 3, 4):
        zu.wait(step - 1)
        zu.start(step)
        zd.wait(step - 1)
        zd.start(step)
    zu.wait(4)
    assemble(z_u, w_u)
    yu.start(1)
    su[0](0)
    zd.wait(4)
    assemble(z_d, w_d)
    yd.start(1)
    sd[0](0)
    ya.wait(2)
    sa[0](2)
    yi.wait(2)

    old_copy.wait()
    n_slots = 8
    wanted = jnp.concatenate([ids_out[i, tens] for i in range(N_Y)], axis=0)
    owners = jnp.floor(wanted * (1.0 / 1024))
    lists = wanted - owners * 1024.0
    own = (owners == dp.astype(F32)).astype(F32)
    one = lax.broadcasted_iota(jnp.int32, (64, 64), 0)
    two = lax.broadcasted_iota(jnp.int32, (64, 64), 1)
    earlier = ((one > two) & (one // 16 == two // 16)).astype(BF16)
    rank = jnp.dot(earlier, own.astype(BF16), preferred_element_type=F32)
    hots = []
    for r in range(2):
        named = jnp.where((own > 0.5) & (rank == float(r)), lists + 1.0, 0.0)
        named = jnp.sum(named.reshape(N_Y, 16, 128), axis=1) - 1.0
        hots.append(named)
    named = jnp.concatenate(hots, axis=0)
    places = lax.broadcasted_iota(jnp.int32, (n_slots, 1024), 1).astype(F32)
    hot = places == named[:, 0:1]
    mine_rows[:, 0:D] = pick(hot.astype(F32).astype(BF16), old_buf[...])
    mine_rows[:, D : D + 128] = jnp.broadcast_to(
        jnp.sum(jnp.where(hot, weight_ref[...], 0.0), axis=1, keepdims=True), (n_slots, 128)
    )
    turn_numbers = [sems.take() for _ in range(N_Y)]
    turn_to = [((lax.rem(y + k, N_Y)) * N_Z + tens, z) for k in range(N_Y)]
    for k in range(1, N_Y):
        sems.send(mine_rows, turn_numbers[k], turn_to[k], dst=owner_rows.at[y])
    @pl.when(jnp.logical_not(is_turn_self))
    def _():
        copy = sems._copy(mine_rows, owner_rows.at[y], turn_numbers[0], turn_to[0])
        copy.start()
        copy.wait_send()
        sems.arrived(owner_rows.at[y], turn_numbers[0], turn_to[0])

    @pl.when(is_turn_self)
    def _():
        owner_rows[y] = mine_rows[...]
    for k in range(1, N_Y):
        sems.arrived(
            owner_rows.at[lax.rem(y + N_Y - k, N_Y)], turn_numbers[k], turn_to[k]
        )
    for r in range(2):
        for i in range(N_Y):
            rows_out[tens, r * N_Y + i : r * N_Y + i + 1, :] = owner_rows[
                i, pl.ds(r * N_Y + y, 1), :
            ]
    row_numbers = [sems.take() for _ in range(7)]
    for k in range(1, 8):
        sems.send(rows_out.at[tens], row_numbers[k - 1], peers[k - 1])

    yu.wait(1)
    yu.start(2)
    su[0](1)
    su[0](3)
    yd.wait(1)
    yd.start(2)
    sd[0](1)
    sd[0](3)
    yu.wait(2)
    su[0](2)
    yd.wait(2)
    sd[0](2)
    for i in range(N_Y):
        sa[1](i)

    for c in range(2):
        for k in range(3):
            part = jnp.dot(x_ref[...], w_a[c * 4 + k], preferred_element_type=F32).astype(BF16)
            if k == 0:
                part = part * 0.125
            qkv[c * 3 + k] = part
    lane = lax.broadcasted_iota(jnp.int32, (1, 128), 1)
    low = (lane < 64).astype(F32).astype(BF16)
    halves = (low, 1 - low)
    key_at = lax.broadcasted_iota(jnp.int32, (1, L), 1)
    for p in range(2):
        keys_ok = key_at < lens_ref[2 * tens + p]
        tokens = slice(p * L, (p + 1) * L)
        for c in range(2):
            for j in range(3):
                columns = slice(j * 128, (j + 1) * 128)
                q = qkv[c * 3, tokens, columns]
                k = qkv[c * 3 + 1, tokens, columns]
                v = qkv[c * 3 + 2, tokens, columns]
                total = None
                for half in halves:
                    scores = lax.dot_general(
                        q * half, k, (((1,), (1,)), ((), ())), preferred_element_type=F32
                    )
                    scores = jnp.where(keys_ok, scores, -1e30)
                    powers = jnp.exp(scores - jnp.max(scores, axis=1, keepdims=True))
                    scale = 1.0 / jnp.sum(powers, axis=1, keepdims=True)
                    probs = (powers * scale).astype(BF16)
                    part = jnp.dot(probs, v * half, preferred_element_type=F32)
                    total = part if total is None else total + part
                ctx[tokens, c * SLAB + j * 128 : c * SLAB + (j + 1) * 128] = total.astype(BF16)
    for b in range(2):
        tokens = slice(b * L, (b + 1) * L)
        mixed = jnp.concatenate(
            [
                jnp.dot(ctx[tokens, :], w_a[c * 4 + 3], preferred_element_type=F32)
                for c in range(2)
            ],
            axis=1,
        )
        values = x_ref[tokens, :].astype(F32) + mixed
        centered = values - jnp.mean(values, axis=1, keepdims=True)
        spread = jnp.mean(centered * centered, axis=1, keepdims=True)
        normed = centered * lax.rsqrt(spread + EPS) * gain_one_ref[...] + shift_one_ref[...]
        first[tokens, :] = normed.astype(BF16)
        acc[tokens, :] = normed.astype(BF16).astype(F32)

    for i in range(N_Y):
        su[1](i)
        sd[1](i)

    def slab(s, carry):
        for b in range(2):
            tokens = slice(b * L, (b + 1) * L)
            up = jnp.dot(first[tokens, :], w_u[s], preferred_element_type=F32)
            act = (0.5 * up * (1.0 + lax.erf(up * (0.5**0.5)))).astype(BF16)
            acc[tokens, :] += lax.dot_general(
                act, w_d[s], (((1,), (1,)), ((), ())), preferred_element_type=F32
            )
        return carry

    lax.fori_loop(0, 8, slab, 0)

    token_at = lax.broadcasted_iota(jnp.int32, (L, 1), 0)
    for p in range(2):
        length = lens_ref[2 * tens + p]
        values = acc[p * L : (p + 1) * L, :]
        centered = values - jnp.mean(values, axis=1, keepdims=True)
        spread = jnp.mean(centered * centered, axis=1, keepdims=True)
        scaled = centered * lax.rsqrt(spread + EPS)
        pooled = jnp.sum(jnp.where(token_at < length, scaled, 0.0), axis=0, keepdims=True)
        emb = pooled / length.astype(F32) * gain_two_ref[...] + shift_two_ref[...]
        emb_group[tens, p : p + 1, :] = emb

    group_numbers = [sems.take() for _ in range(7)]
    for k in range(1, 8):
        sems.send(emb_group.at[tens], group_numbers[k - 1], peers[k - 1])
    for k in range(1, 8):
        other = lax.rem(tens + 8 - k, 8)
        sems.arrived(emb_group.at[other], group_numbers[k - 1], peers[k - 1])
    for t in range(8):
        both = emb_group[t]
        @pl.when(core == 0)
        def _():
            emb_out[0, y, z, 2 * t : 2 * t + 2, :] = both[:, :SLAB]
        @pl.when(core == 1)
        def _():
            emb_out[1, y, z, 2 * t : 2 * t + 2, :] = both[:, SLAB:]
    ze = Ring(
        sems, N_Z, z, z_right, z_left,
        lambda i: emb_out.at[core, y, i],
        lambda i: (emb_out.at[core, y, i, pl.ds(0, 8)], emb_out.at[core, y, i, pl.ds(8, 8)]),
    )
    ye = Ring(
        sems, N_Y, y, y_right, y_left,
        lambda i: emb_out.at[core, i],
        lambda i: (emb_out.at[core, i, pl.ds(0, 4)], emb_out.at[core, i, pl.ds(4, 4)]),
    )
    for step in range(1, 5):
        ze.start(step)
        ze.wait(step)
    numbers = [sems.take() for _ in range(N_Y)]
    ye.start(1)
    sems.send(emb_out.at[core, y], numbers[0], sibling)
    ye.wait(1)
    ye.start(2)
    for k in (1, 3):
        sems.send(emb_out.at[core, lax.rem(y + k, N_Y)], numbers[k], sibling)
    ye.wait(2)
    sems.send(emb_out.at[core, lax.rem(y + 2, N_Y)], numbers[2], sibling)
    for k in range(N_Y):
        sems.arrived(emb_out.at[1 - core, lax.rem(y + k, N_Y)], numbers[k], sibling)

    for k in range(1, 8):
        origin = lax.rem(tens + 8 - k, 8)
        place = pl.ds(pl.multiple_of(origin * 96, 32), 96)
        sems.arrived(rot_out.at[place], rot_numbers[k - 1], peers[k - 1])
        sems.arrived(rows_out.at[origin], row_numbers[k - 1], peers[k - 1])
    sems.finish()


def finish_kernel(emb_ref, ids_ref, rows_ref, rot_ref, weight_ref, old_ref, rotated_ref, centroids_ref, ids_row):
    step = pl.program_id(0)
    dp = lax.axis_index("dp")

    @pl.when(step == 0)
    def _():
        ids_row[...] = jnp.transpose(ids_ref[...])[0:8, :]
        ids = ids_ref[pl.ds(pl.multiple_of(dp * 16, 16), 16), :]
        owners = jnp.floor(ids * (1.0 / 1024))
        owner_y = jnp.floor(owners * (1.0 / N_Z))
        owner_z = owners - owner_y * N_Z
        one = lax.broadcasted_iota(jnp.int32, (16, 16), 0)
        two = lax.broadcasted_iota(jnp.int32, (16, 16), 1)
        owners_row = jnp.sum(jnp.where(one == two, owners[:, 0:16], 0.0), axis=0, keepdims=True)
        rank = jnp.sum(
            ((owners[:, 0:16] == owners_row) & (two < one)).astype(F32), axis=1, keepdims=True
        )
        place = owner_z * 8.0 + rank * N_Y + owner_y
        spots = lax.broadcasted_iota(jnp.int32, (16, 64), 1).astype(F32)
        hot = (place[:, 0:64] == spots).astype(F32).astype(BF16)
        old = pick(hot, rows_ref[...])
        same = ids[:, 0:1] == ids_row[0:1, :]
        counts = jnp.sum(same.astype(F32), axis=1, keepdims=True)
        same = same.astype(F32).astype(BF16)
        weight = old[:, D : D + 1]
        result = None
        for h in range(2):
            sums = pick(same, emb_ref[h])
            centroids = (weight * old[:, h * SLAB : (h + 1) * SLAB] + sums) / (weight + counts)
            resid = emb_ref[h, pl.ds(pl.multiple_of(dp * 16, 16), 16), :] - centroids
            part = jnp.dot(
                resid,
                rot_ref[h * SLAB : (h + 1) * SLAB, :],
                precision=lax.Precision.HIGHEST,
                preferred_element_type=F32,
            )
            result = part if result is None else result + part
        rotated_ref[...] = result

    one = lax.broadcasted_iota(jnp.int32, (128, 128), 0)
    two = lax.broadcasted_iota(jnp.int32, (128, 128), 1)
    weight = jnp.sum(
        jnp.where(one == two, weight_ref[pl.ds(step, 1), :], 0.0), axis=1, keepdims=True
    )
    number = lax.broadcasted_iota(jnp.int32, (128, ROWS), 0) + dp * 1024 + step * 128
    hot = number.astype(F32) == ids_row[0:1, :]
    counts = jnp.sum(hot.astype(F32), axis=1, keepdims=True)
    hot = hot.astype(F32).astype(BF16)
    for h in range(2):
        columns = slice(h * SLAB, (h + 1) * SLAB)
        sums = pick(hot, emb_ref[h])
        centroids_ref[:, columns] = (weight * old_ref[:, columns] + sums) / (weight + counts)


VMEM = pl.BlockSpec(memory_space=pltpu.VMEM)
SMEM = pl.BlockSpec(memory_space=pltpu.SMEM)
ANY = pl.BlockSpec(memory_space=pl.ANY)


def local(
    hidden,
    lengths,
    owner_of,
    list_local,
    old_weight,
    old_centroids,
    w_qkv,
    w_out,
    gain_one,
    shift_one,
    w_up,
    w_down,
    gain_two,
    shift_two,
    rotation,
):
    lists = owner_of[:, 0] * 1024 + list_local
    ids = jnp.broadcast_to(lists.astype(F32)[:, None], (16, 128))
    weight = old_weight.astype(F32)
    vmem = pltpu.VMEM
    emb, ids, rows, rot = pl.pallas_call(
        encode_kernel,
        out_shape=(
            jax.ShapeDtypeStruct((2, N_Y, N_Z, 16, SLAB), F32),
            jax.ShapeDtypeStruct((N_Y, N_Z, 16, 128), F32),
            jax.ShapeDtypeStruct((8, 8, D + 128), F32),
            jax.ShapeDtypeStruct((D, 96), F32),
        ),
        in_specs=[VMEM, SMEM, VMEM, VMEM, ANY] + [VMEM] * 9,
        out_specs=(VMEM,) * 4,
        scratch_shapes=[
            vmem((8, D, SLAB), BF16),
            vmem((8, D, SLAB), BF16),
            vmem((8, D, SLAB), BF16),
            vmem((N_Z, 4, 24, SLAB), BF16),
            vmem((N_Z, 4, 24, SLAB), BF16),
            vmem((N_Z, 4, 24, SLAB), BF16),
            vmem((192, SLAB), F32),
            vmem((1024, D), F32),
            vmem((8, 96, 96), F32),
            vmem((8, D + 128), F32),
            vmem((N_Y, 8, D + 128), F32),
            vmem((8, 2, D), F32),
            vmem((6, ROWS, SLAB), BF16),
            vmem((ROWS, D), BF16),
            vmem((ROWS, D), BF16),
            vmem((ROWS, D), F32),
            pltpu.SemaphoreType.DMA((N_COPIES,)),
            pltpu.SemaphoreType.DMA((N_COPIES,)),
            pltpu.SemaphoreType.DMA((1,)),
        ],
        compiler_params=pltpu.CompilerParams(
            collective_id=0, has_side_effects=True, vmem_limit_bytes=50 * 2**20
        ),
    )(
        hidden.reshape(ROWS, D),
        lengths,
        ids,
        weight.reshape(1, 1024),
        old_centroids,
        w_qkv,
        w_out,
        gain_one.reshape(1, D),
        shift_one.reshape(1, D),
        w_up,
        w_down.T,
        gain_two.reshape(1, D),
        shift_two.reshape(1, D),
        rotation,
    )
    whole = lambda *shape: pl.BlockSpec(shape, lambda i: (0,) * len(shape))
    return pl.pallas_call(
        finish_kernel,
        grid=(8,),
        out_shape=(
            jax.ShapeDtypeStruct((16, 96), F32),
            jax.ShapeDtypeStruct((1024, D), F32),
        ),
        in_specs=[
            whole(2, ROWS, SLAB),
            whole(ROWS, 128),
            whole(64, D + 128),
            whole(D, 96),
            whole(8, 128),
            pl.BlockSpec((128, D), lambda i: (i, 0)),
        ],
        out_specs=(whole(16, 96), pl.BlockSpec((128, D), lambda i: (i, 0))),
        scratch_shapes=[vmem((8, ROWS), F32)],
        compiler_params=pltpu.CompilerParams(vmem_limit_bytes=40 * 2**20),
    )(
        emb.reshape(2, ROWS, SLAB),
        ids.reshape(ROWS, 128),
        rows.reshape(64, D + 128),
        rot,
        weight.reshape(8, 128),
        old_centroids,
    )


def solution(mesh):
    return jax.shard_map(
        local,
        mesh=mesh,
        in_specs=(
            P(("dp", "tensor"), None, None),
            P("dp"),
            P("dp", None),
            P("dp"),
            P("dp"),
            P("dp", None),
            P("dp", None),
            P("dp", None),
            P(),
            P(),
            P("dp", "tensor"),
            P("tensor", "dp"),
            P(),
            P(),
            P("tensor", None),
        ),
        out_specs=(P("dp", "tensor"), P("dp", None)),
        check_vma=False,
    )
```

```python
import functools

import jax
import jax.numpy as jnp
from jax import lax
from jax.experimental import pallas as pl
from jax.experimental.pallas import tpu as pltpu
from jax.sharding import PartitionSpec as P

EPS = 1e-05
MESH = pl.DeviceIdType.MESH
F32 = jnp.float32
BF16 = jnp.bfloat16

L = 256
D = 768
SLAB = 384
N_Y = 4
N_Z = 8
N_X = 4
ROWS = 512


def split3(values):
    high = values.astype(BF16)
    rest = values - high.astype(F32)
    mid = rest.astype(BF16)
    low = (rest - mid.astype(F32)).astype(BF16)
    return high, mid, low


def pick(hot, values):
    parts = split3(values)
    return sum(jnp.dot(hot, part, preferred_element_type=F32) for part in parts)


class Ring:
    def __init__(self, sems, n, me, right, left, parts):
        self.n, self.me, self.right, self.left = n, me, right, left
        self.parts = parts
        self.sems = sems
        self.ids = [[(sems.take(), sems.take()) for _ in range(2)] for _ in range(n // 2)]

    def _at(self, offset):
        return lax.rem(self.me + offset + self.n, self.n)

    def start(self, step, part):
        a, b = self.ids[step - 1][part]
        last = step == self.n // 2
        if not last or part == 0:
            self.sems.send(self.parts(self._at(1 - step))[part], a, self.right)
        if not last or part == 1:
            self.sems.send(self.parts(self._at(step - 1))[part], b, self.left)

    def wait(self, step, part):
        a, b = self.ids[step - 1][part]
        last = step == self.n // 2
        if not last or part == 0:
            self.sems.arrived(self.parts(self._at(-step))[part], a, self.right)
        if not last or part == 1:
            self.sems.arrived(self.parts(self._at(step))[part], b, self.left)

    def begin(self):
        for part in range(2):
            self.start(1, part)

    def advance(self, step):
        for part in range(2):
            self.wait(step, part)
            if step < self.n // 2:
                self.start(step + 1, part)


class Direct:
    def __init__(self, sems, n, me, device, block):
        self.sems, self.n, self.me, self.device, self.block = sems, n, me, device, block
        self.numbers = [sems.take() for _ in range(n)]

    def begin(self):
        offsets = sorted(range(1, self.n), key=lambda k: -min(k, self.n - k))
        for k in offsets:
            i = lax.rem(self.me + k, self.n)
            self.sems.send(self.block(self.me), self.numbers[k], self.device(i))

    def done(self):
        for k in range(1, self.n):
            i = lax.rem(self.me + self.n - k, self.n)
            self.sems.arrived(self.block(i), self.numbers[k], self.device(i))


class Copies:
    def __init__(self, send, recv):
        self.send_sems, self.recv_sems = send, recv
        self.count = 0
        self.started = []

    def take(self):
        self.count += 1
        return self.count - 1

    def _copy(self, src, dst, number, device):
        return pltpu.make_async_remote_copy(
            src_ref=src,
            dst_ref=dst,
            send_sem=self.send_sems.at[number],
            recv_sem=self.recv_sems.at[number],
            device_id=device,
            device_id_type=MESH,
        )

    def send(self, src, number, device, dst=None):
        copy = self._copy(src, src if dst is None else dst, number, device)
        copy.start()
        self.started.append(copy)

    def arrived(self, ref, number, device):
        self._copy(ref, ref, number, device).wait_recv()

    def finish(self):
        for copy in self.started:
            copy.wait_send()
        self.started = []


N_COPIES = 288


class Spread(Ring):
    def __init__(self, sems, n, me, right, left, sibling, mine, theirs):
        super().__init__(sems, n, me, right, left, mine)
        self.sibling, self.theirs = sibling, theirs
        self.hands = [(sems.take(), sems.take()) for _ in range(n)]

    def _hand(self, offset, part):
        number = self.hands[offset % self.n][part]
        self.sems.send(self.parts(self._at(offset))[part], number, self.sibling)

    def begin_part(self, part):
        self.start(1, part)
        self._hand(0, part)

    def begin(self):
        for part in range(2):
            self.begin_part(part)

    def advance(self, step):
        for part in range(2):
            self.wait(step, part)
            if step < self.n // 2:
                self.start(step + 1, part)
                self._hand(-step, part)
            self._hand(step, part)

    def done(self):
        for offset in range(self.n):
            for part in range(2):
                i = self._at(offset)
                self.sems.arrived(self.theirs(i)[part], self.hands[offset][part], self.sibling)


def encode_kernel(
    lens_ref,
    owner_ref,
    list_ref,
    weight_ref,
    gain_one_ref,
    shift_one_ref,
    gain_two_ref,
    shift_two_ref,
    x_any,
    old_ref,
    wqkv_ref,
    wout_ref,
    wup_ref,
    wdown_ref,
    rot_ref,
    emb_out,
    ids_out,
    rows_out,
    rot_out,
    w_a,
    w_u,
    w_d,
    z_a,
    y_k,
    y_u,
    z_d,
    turned,
    x_ref,
    x_turned,
    rot_buf,
    old_buf,
    rot_send,
    mine_rows,
    owner_rows,
    emb_group,
    qkv,
    ctx,
    first,
    act,
    acc,
    send_sems,
    recv_sems,
    local_sems,
):
    dp = lax.axis_index("dp")
    tens = lax.axis_index("tensor")
    y, z = dp // N_Z, lax.rem(dp, N_Z)
    x, core = tens // 2, lax.rem(tens, 2)

    def at_y(i):
        return (i * N_Z + z, tens)

    def at_z(i):
        return (y * N_Z + i, tens)

    y_right, y_left = at_y(lax.rem(y + 1, N_Y)), at_y(lax.rem(y + N_Y - 1, N_Y))
    z_right, z_left = at_z(lax.rem(z + 1, N_Z)), at_z(lax.rem(z + N_Z - 1, N_Z))
    peers = [(dp, lax.rem(tens + k, 8)) for k in range(1, 8)]
    sibling = (dp, 2 * x + 1 - core)
    is_turn_self = tens == z
    turn = [(i * N_Z + tens, z) for i in range(N_Y)]

    barrier = pltpu.get_barrier_semaphore()
    others = [at_y(lax.rem(y + k, N_Y)) for k in range(1, N_Y)]
    others += [at_z(lax.rem(z + k, N_Z)) for k in range(1, N_Z)]
    for device in others + peers:
        pl.semaphore_signal(barrier, inc=1, device_id=device, device_id_type=MESH)
    for i in range(N_Y):
        @pl.when(jnp.logical_not(jnp.logical_and(is_turn_self, y == i)))
        def _():
            pl.semaphore_signal(barrier, inc=1, device_id=turn[i], device_id_type=MESH)

    def cut(ref, at):
        return ref.at[:, pl.ds(pl.multiple_of(at * SLAB, 128), SLAB)]

    loads = [
        (cut(wqkv_ref, core), z_a.at[z, 0]),
        (cut(wqkv_ref, 4 + core), z_a.at[z, 1]),
        (cut(wout_ref, core), z_d.at[z, 4]),
        (cut(wqkv_ref, 2 + core), y_k.at[y]),
        (wup_ref, y_u.at[y, x]),
        (wdown_ref, z_d.at[z, x]),
        (x_any, x_ref),
        (rot_ref, rot_buf),
        (old_ref, old_buf),
    ]
    loads = [
        pltpu.make_async_copy(src, dst, local_sems.at[i]) for i, (src, dst) in enumerate(loads)
    ]
    for load in loads:
        load.start()
    ids_rows = [
        jnp.full((1, 128), owner_ref[i] * 1024 + list_ref[i], jnp.int32) for i in range(16)
    ]
    ids_out[y, z] = jnp.concatenate(ids_rows, axis=0).astype(F32)
    for load in loads[:6]:
        load.wait()
    pl.semaphore_wait(barrier, 17 + N_Y - is_turn_self.astype(jnp.int32))

    sems = Copies(send_sems, recv_sems)

    def z_rows(i):
        return pl.ds(pl.multiple_of(i * 96, 32), 96)

    def y_rows(i):
        return pl.ds(pl.multiple_of(i * 192, 64), 192)

    def y_last(buf, start, count):
        half = count // 2

        def parts(c, i):
            if half:
                return [
                    buf.at[pl.ds(c * 4 + start + k, half), y_rows(i)] for k in (0, half)
                ]
            return [
                buf.at[c * 4 + start, pl.ds(pl.multiple_of(i * 192 + k, 32), 96)] for k in (0, 96)
            ]

        return Spread(
            sems, N_Y, y, y_right, y_left, sibling,
            lambda i: parts(core, i), lambda i: parts(1 - core, i),
        )

    def z_last(buf, start, count):
        half = count // 2

        def parts(c, i):
            if half:
                return [
                    buf.at[pl.ds(c * 4 + start + k, half), z_rows(i)] for k in (0, half)
                ]
            return [
                buf.at[c * 4 + start, pl.ds(pl.multiple_of(i * 96 + k, 16), 48)] for k in (0, 48)
            ]

        return Spread(
            sems, N_Z, z, z_right, z_left, sibling,
            lambda i: parts(core, i), lambda i: parts(1 - core, i),
        )

    def assemble(blocks, full, at, rows):
        for i, block in enumerate(blocks):
            turned[i * 24 : (i + 1) * 24, :] = block.astype(F32)
        full[at, rows, :] = turned[0 : 24 * len(blocks), :].astype(BF16)

    az = Direct(sems, N_Z, z, at_z, lambda i: z_a.at[i])
    ky = Direct(sems, N_Y, y, at_y, lambda i: y_k.at[i])
    uy = Direct(sems, N_Y, y, at_y, lambda i: y_u.at[i])
    iz = Direct(sems, N_Z, z, at_z, lambda i: ids_out.at[y, i])
    iy = Direct(sems, N_Y, y, at_y, lambda i: ids_out.at[i])
    dz = Ring(
        sems, N_Z, z, z_right, z_left,
        lambda i: (z_d.at[i, pl.ds(0, 2)], z_d.at[i, pl.ds(2, 3)]),
    )
    qv, o, k_z = y_last(w_a, 0, 2), y_last(w_a, 2, 1), z_last(w_a, 3, 1)
    u_z, d_y = z_last(w_u, 0, 4), y_last(w_d, 0, 4)

    az.begin()
    ky.begin()
    x_numbers = [(sems.take(), sems.take()) for _ in range(3)]
    for at, buf in enumerate((y_u.at[y, x], z_d.at[z, x])):
        for k in range(1, 4):
            sems.send(buf, x_numbers[k - 1][at], (dp, lax.rem(tens + 2 * k, 8)))

    def along_x(buf, at):
        for k in range(1, 4):
            origin = lax.rem(x + N_X - k, N_X)
            sems.arrived(
                buf.at[origin], x_numbers[k - 1][at], (dp, lax.rem(tens + 2 * k, 8))
            )

    iz.begin()
    ky.done()
    assemble([y_k[i] for i in range(N_Y)], w_a, core * 4 + 3, z_rows(z))
    k_z.begin()
    along_x(y_u.at[y], 0)
    uy.begin()
    along_x(z_d.at[z], 1)
    dz.begin()
    az.done()
    for s in range(2):
        assemble([z_a[i, s] for i in range(N_Z)], w_a, core * 4 + s, y_rows(y))
        qv.begin_part(s)
    k_z.advance(1)
    dz.advance(1)
    uy.done()
    for s in range(4):
        assemble([y_u[i, s] for i in range(N_Y)], w_u, core * 4 + s, z_rows(z))
    k_z.advance(2)
    dz.advance(2)
    u_z.begin()
    iz.done()
    iy.begin()

    for load in loads[6:]:
        load.wait()
    column = lax.broadcasted_iota(jnp.int32, (1, D), 1)
    by_z = column // 96
    by_y = (column - by_z * 96) // 24
    source = by_y * 192 + by_z * 24 + (column - by_z * 96 - by_y * 24)
    order = lax.broadcasted_iota(jnp.int32, (D, D), 0) == source
    order = order.astype(F32).astype(BF16)
    x_turned[...] = jnp.dot(x_ref[...], order, preferred_element_type=F32).astype(BF16)

    k_z.advance(3)
    dz.advance(3)
    for k in range(8):
        rot_send[k] = rot_buf[:, k * 96 : (k + 1) * 96]
    k_z.advance(4)
    dz.advance(4)
    for s in range(5):
        full, at = (w_a, core * 4 + 2) if s == 4 else (w_d, core * 4 + s)
        assemble([z_d[i, s] for i in range(N_Z)], full, at, y_rows(y))
    qv.advance(1)
    d_y.begin()
    u_z.advance(1)
    iy.done()

    n_slots = 8
    wanted = jnp.concatenate([ids_out[i, tens] for i in range(N_Y)], axis=0)
    owners = jnp.floor(wanted * (1.0 / 1024))
    lists = wanted - owners * 1024.0
    own = (owners == dp.astype(F32)).astype(F32)
    one = lax.broadcasted_iota(jnp.int32, (64, 64), 0)
    two = lax.broadcasted_iota(jnp.int32, (64, 64), 1)
    earlier = ((one > two) & (one // 16 == two // 16)).astype(BF16)
    rank = jnp.dot(earlier, own.astype(BF16), preferred_element_type=F32)
    hots = []
    for r in range(2):
        named = jnp.where((own > 0.5) & (rank == float(r)), lists + 1.0, 0.0)
        named = jnp.sum(named.reshape(N_Y, 16, 128), axis=1) - 1.0
        hots.append(named)
    named = jnp.concatenate(hots, axis=0)
    places = lax.broadcasted_iota(jnp.int32, (n_slots, 1024), 1).astype(F32)
    hot = places == named[:, 0:1]
    mine_rows[:, 0:D] = pick(hot.astype(F32).astype(BF16), old_buf[...])
    mine_rows[:, D : D + 128] = jnp.broadcast_to(
        jnp.sum(
            jnp.where(hot, weight_ref[...].astype(F32).reshape(1, 1024), 0.0),
            axis=1,
            keepdims=True,
        ),
        (n_slots, 128),
    )
    qv.advance(2)
    o.begin()
    u_z.advance(2)
    qv.done()
    k_z.done()

    turn_numbers = [sems.take() for _ in range(N_Y)]
    turn_to = [((lax.rem(y + k, N_Y)) * N_Z + tens, z) for k in range(N_Y)]
    rot_numbers = [sems.take() for _ in range(7)]
    row_numbers = [sems.take() for _ in range(7)]
    rot_place = pl.ds(pl.multiple_of(tens * 96, 32), 96)

    def send_rows_and_rotation():
        for k in range(1, N_Y):
            sems.send(mine_rows, turn_numbers[k], turn_to[k], dst=owner_rows.at[y])

        @pl.when(jnp.logical_not(is_turn_self))
        def _():
            copy = sems._copy(mine_rows, owner_rows.at[y], turn_numbers[0], turn_to[0])
            copy.start()
            copy.wait_send()

        @pl.when(is_turn_self)
        def _():
            owner_rows[y] = mine_rows[...]

        rot_out[rot_place, :] = rot_send[tens]
        for k in range(1, 8):
            other = lax.rem(tens + k, 8)
            sems.send(
                rot_send.at[other], rot_numbers[k - 1], peers[k - 1], dst=rot_out.at[rot_place]
            )

    def share_rows():
        @pl.when(jnp.logical_not(is_turn_self))
        def _():
            sems.arrived(owner_rows.at[y], turn_numbers[0], turn_to[0])

        for k in range(1, N_Y):
            sems.arrived(
                owner_rows.at[lax.rem(y + N_Y - k, N_Y)], turn_numbers[k], turn_to[k]
            )
        for r in range(2):
            for i in range(N_Y):
                rows_out[tens, r * N_Y + i : r * N_Y + i + 1, :] = owner_rows[
                    i, pl.ds(r * N_Y + y, 1), :
                ]
        for k in range(1, 8):
            sems.send(rows_out.at[tens], row_numbers[k - 1], peers[k - 1])

    def project(c):
        for at, source in ((0, x_ref), (1, x_ref), (3, x_turned)):
            part = jnp.dot(source[...], w_a[c * 4 + at], preferred_element_type=F32).astype(BF16)
            if at == 0:
                part = part * 0.125
            qkv[c * 3 + min(at, 2)] = part

    lane = lax.broadcasted_iota(jnp.int32, (1, 128), 1)
    low = (lane < 64).astype(F32).astype(BF16)
    both_halves = (low, 1 - low)
    key_at = lax.broadcasted_iota(jnp.int32, (1, L), 1)

    def attend(p, c, j):
        keys_ok = key_at < lens_ref[2 * tens + p]
        tokens = slice(p * L, (p + 1) * L)
        columns = slice(j * 128, (j + 1) * 128)
        q = qkv[c * 3, tokens, columns]
        v = qkv[c * 3 + 1, tokens, columns]
        k = qkv[c * 3 + 2, tokens, columns]
        total = None
        for half in both_halves:
            scores = lax.dot_general(
                q * half, k, (((1,), (1,)), ((), ())), preferred_element_type=F32
            )
            scores = jnp.where(keys_ok, scores, -1e30)
            powers = jnp.exp(scores - jnp.max(scores, axis=1, keepdims=True))
            scale = 1.0 / jnp.sum(powers, axis=1, keepdims=True)
            probs = (powers * scale).astype(BF16)
            part = jnp.dot(probs, v * half, preferred_element_type=F32)
            total = part if total is None else total + part
        ctx[tokens, c * SLAB + j * 128 : c * SLAB + (j + 1) * 128] = total.astype(BF16)

    def mix(b):
        tokens = slice(b * L, (b + 1) * L)
        mixed = jnp.concatenate(
            [
                jnp.dot(ctx[tokens, :], w_a[c * 4 + 2], preferred_element_type=F32)
                for c in range(2)
            ],
            axis=1,
        )
        values = x_ref[tokens, :].astype(F32) + mixed
        centered = values - jnp.mean(values, axis=1, keepdims=True)
        spread = jnp.mean(centered * centered, axis=1, keepdims=True)
        normed = centered * lax.rsqrt(spread + EPS) * gain_one_ref[...].reshape(
            1, D
        ) + shift_one_ref[...].reshape(1, D)
        normed = normed.astype(BF16)
        acc[tokens, :] = normed.astype(F32)
        first[tokens, :] = jnp.dot(normed, order, preferred_element_type=F32).astype(BF16)

    project(0)
    send_rows_and_rotation()
    project(1)
    steps = {
        3: lambda: u_z.advance(3),
        4: lambda: o.advance(1),
        6: share_rows,
        8: lambda: o.advance(2),
        9: lambda: u_z.advance(4),
        10: lambda: d_y.advance(1),
    }
    for n, (c, p, j) in enumerate(
        (c, p, j) for c in range(2) for p in range(2) for j in range(3)
    ):
        attend(p, c, j)
        if n in steps:
            steps[n]()
    o.done()
    mix(0)
    mix(1)
    u_z.done()

    def raise_slab(s, carry):
        for b in range(2):
            tokens = slice(b * L, (b + 1) * L)
            up = jnp.dot(first[tokens, :], w_u[s], preferred_element_type=F32)
            act[s, tokens, :] = (0.5 * up * (1.0 + lax.erf(up * (0.5**0.5)))).astype(BF16)
        return carry

    def lower_slab(s, carry):
        for b in range(2):
            tokens = slice(b * L, (b + 1) * L)
            acc[tokens, :] += lax.dot_general(
                act[s, tokens, :], w_d[s], (((1,), (1,)), ((), ())), preferred_element_type=F32
            )
        return carry

    lax.fori_loop(0, 8, raise_slab, 0)
    d_y.advance(2)
    d_y.done()
    lax.fori_loop(0, 8, lower_slab, 0)

    token_at = lax.broadcasted_iota(jnp.int32, (L, 1), 0)
    for p in range(2):
        length = lens_ref[2 * tens + p]
        values = acc[p * L : (p + 1) * L, :]
        centered = values - jnp.mean(values, axis=1, keepdims=True)
        spread = jnp.mean(centered * centered, axis=1, keepdims=True)
        scaled = centered * lax.rsqrt(spread + EPS)
        pooled = jnp.sum(jnp.where(token_at < length, scaled, 0.0), axis=0, keepdims=True)
        emb = pooled / length.astype(F32) * gain_two_ref[...].reshape(1, D)
        emb_group[tens, p : p + 1, :] = emb + shift_two_ref[...].reshape(1, D)

    group_numbers = [sems.take() for _ in range(7)]
    for k in range(1, 8):
        sems.send(emb_group.at[tens], group_numbers[k - 1], peers[k - 1])
    sems.finish()
    for k in range(1, 8):
        origin = lax.rem(tens + 8 - k, 8)
        place = pl.ds(pl.multiple_of(origin * 96, 32), 96)
        sems.arrived(rot_out.at[place], rot_numbers[k - 1], peers[k - 1])
        sems.arrived(rows_out.at[origin], row_numbers[k - 1], peers[k - 1])
    for k in range(1, 8):
        other = lax.rem(tens + 8 - k, 8)
        sems.arrived(emb_group.at[other], group_numbers[k - 1], peers[k - 1])
    for t in range(8):
        both = emb_group[t]
        @pl.when(core == 0)
        def _():
            emb_out[0, y, z, 2 * t : 2 * t + 2, :] = both[:, :SLAB]
        @pl.when(core == 1)
        def _():
            emb_out[1, y, z, 2 * t : 2 * t + 2, :] = both[:, SLAB:]
    ze = Direct(sems, N_Z, z, at_z, lambda i: emb_out.at[core, y, i])

    def emb_parts(c, i):
        return emb_out.at[c, i, pl.ds(0, 4)], emb_out.at[c, i, pl.ds(4, 4)]

    ye = Spread(
        sems, N_Y, y, y_right, y_left, sibling,
        lambda i: emb_parts(core, i), lambda i: emb_parts(1 - core, i),
    )
    ze.begin()
    ze.done()
    ye.begin()
    ye.advance(1)
    ye.advance(2)
    ye.done()
    sems.finish()


def finish_kernel(emb_ref, ids_ref, rows_ref, rot_ref, weight_ref, old_ref, rotated_ref, centroids_ref, ids_row):
    step = pl.program_id(0)
    dp = lax.axis_index("dp")

    @pl.when(step == 0)
    def _():
        ids_row[...] = jnp.transpose(ids_ref[...])[0:8, :]
        ids = ids_ref[pl.ds(pl.multiple_of(dp * 16, 16), 16), :]
        owners = jnp.floor(ids * (1.0 / 1024))
        owner_y = jnp.floor(owners * (1.0 / N_Z))
        owner_z = owners - owner_y * N_Z
        one = lax.broadcasted_iota(jnp.int32, (16, 16), 0)
        two = lax.broadcasted_iota(jnp.int32, (16, 16), 1)
        owners_row = jnp.sum(jnp.where(one == two, owners[:, 0:16], 0.0), axis=0, keepdims=True)
        rank = jnp.sum(
            ((owners[:, 0:16] == owners_row) & (two < one)).astype(F32), axis=1, keepdims=True
        )
        place = owner_z * 8.0 + rank * N_Y + owner_y
        spots = lax.broadcasted_iota(jnp.int32, (16, 64), 1).astype(F32)
        hot = (place[:, 0:64] == spots).astype(F32).astype(BF16)
        old = pick(hot, rows_ref[...])
        same = ids[:, 0:1] == ids_row[0:1, :]
        counts = jnp.sum(same.astype(F32), axis=1, keepdims=True)
        same = same.astype(F32).astype(BF16)
        weight = old[:, D : D + 1]
        result = None
        for h in range(2):
            sums = pick(same, emb_ref[h])
            centroids = (weight * old[:, h * SLAB : (h + 1) * SLAB] + sums) / (weight + counts)
            resid = emb_ref[h, pl.ds(pl.multiple_of(dp * 16, 16), 16), :] - centroids
            part = jnp.dot(
                resid,
                rot_ref[h * SLAB : (h + 1) * SLAB, :],
                precision=lax.Precision.HIGHEST,
                preferred_element_type=F32,
            )
            result = part if result is None else result + part
        rotated_ref[...] = result

    one = lax.broadcasted_iota(jnp.int32, (128, 128), 0)
    two = lax.broadcasted_iota(jnp.int32, (128, 128), 1)
    weight = jnp.sum(
        jnp.where(one == two, weight_ref[pl.ds(step, 1), :], 0.0), axis=1, keepdims=True
    )
    number = lax.broadcasted_iota(jnp.int32, (128, ROWS), 0) + dp * 1024 + step * 128
    hot = number.astype(F32) == ids_row[0:1, :]
    counts = jnp.sum(hot.astype(F32), axis=1, keepdims=True)
    hot = hot.astype(F32).astype(BF16)
    for h in range(2):
        columns = slice(h * SLAB, (h + 1) * SLAB)
        sums = pick(hot, emb_ref[h])
        centroids_ref[:, columns] = (weight * old_ref[:, columns] + sums) / (weight + counts)


VMEM = pl.BlockSpec(memory_space=pltpu.VMEM)
SMEM = pl.BlockSpec(memory_space=pltpu.SMEM)
ANY = pl.BlockSpec(memory_space=pl.ANY)


def local(
    hidden,
    lengths,
    owner_of,
    list_local,
    old_weight,
    old_centroids,
    w_qkv,
    w_out,
    gain_one,
    shift_one,
    w_up,
    w_down,
    gain_two,
    shift_two,
    rotation,
):
    weight = old_weight.astype(F32)
    vmem = pltpu.VMEM
    emb, ids, rows, rot = pl.pallas_call(
        encode_kernel,
        out_shape=(
            jax.ShapeDtypeStruct((2, N_Y, N_Z, 16, SLAB), F32),
            jax.ShapeDtypeStruct((N_Y, N_Z, 16, 128), F32),
            jax.ShapeDtypeStruct((8, 8, D + 128), F32),
            jax.ShapeDtypeStruct((D, 96), F32),
        ),
        in_specs=[SMEM] * 3 + [VMEM] * 5 + [ANY] * 7,
        out_specs=(VMEM,) * 4,
        scratch_shapes=[
            vmem((8, D, SLAB), BF16),
            vmem((8, D, SLAB), BF16),
            vmem((8, D, SLAB), BF16),
            vmem((N_Z, 2, 24, SLAB), BF16),
            vmem((N_Y, 24, SLAB), BF16),
            vmem((N_Y, 4, 24, SLAB), BF16),
            vmem((N_Z, 5, 24, SLAB), BF16),
            vmem((192, SLAB), F32),
            vmem((ROWS, D), BF16),
            vmem((ROWS, D), BF16),
            vmem((96, D), F32),
            vmem((1024, D), F32),
            vmem((8, 96, 96), F32),
            vmem((8, D + 128), F32),
            vmem((N_Y, 8, D + 128), F32),
            vmem((8, 2, D), F32),
            vmem((6, ROWS, SLAB), BF16),
            vmem((ROWS, D), BF16),
            vmem((ROWS, D), BF16),
            vmem((8, ROWS, SLAB), BF16),
            vmem((ROWS, D), F32),
            pltpu.SemaphoreType.DMA((N_COPIES,)),
            pltpu.SemaphoreType.DMA((N_COPIES,)),
            pltpu.SemaphoreType.DMA((9,)),
        ],
        compiler_params=pltpu.CompilerParams(
            collective_id=0, has_side_effects=True, vmem_limit_bytes=60 * 2**20
        ),
    )(
        lengths,
        owner_of.reshape(16),
        list_local,
        old_weight,
        gain_one,
        shift_one,
        gain_two,
        shift_two,
        hidden.reshape(ROWS, D),
        old_centroids,
        w_qkv,
        w_out,
        w_up,
        w_down.T,
        rotation,
    )
    whole = lambda *shape: pl.BlockSpec(shape, lambda i: (0,) * len(shape))
    return pl.pallas_call(
        finish_kernel,
        grid=(8,),
        out_shape=(
            jax.ShapeDtypeStruct((16, 96), F32),
            jax.ShapeDtypeStruct((1024, D), F32),
        ),
        in_specs=[
            whole(2, ROWS, SLAB),
            whole(ROWS, 128),
            whole(64, D + 128),
            whole(D, 96),
            whole(8, 128),
            pl.BlockSpec((128, D), lambda i: (i, 0)),
        ],
        out_specs=(whole(16, 96), pl.BlockSpec((128, D), lambda i: (i, 0))),
        scratch_shapes=[vmem((8, ROWS), F32)],
        compiler_params=pltpu.CompilerParams(vmem_limit_bytes=40 * 2**20),
    )(
        emb.reshape(2, ROWS, SLAB),
        ids.reshape(ROWS, 128),
        rows.reshape(64, D + 128),
        rot,
        weight.reshape(8, 128),
        old_centroids,
    )


def solution(mesh):
    return jax.shard_map(
        local,
        mesh=mesh,
        in_specs=(
            P(("dp", "tensor"), None, None),
            P("dp"),
            P("dp", None),
            P("dp"),
            P("dp"),
            P("dp", None),
            P("dp", None),
            P("dp", None),
            P(),
            P(),
            P("dp", "tensor"),
            P("tensor", "dp"),
            P(),
            P(),
            P("tensor", None),
        ),
        out_specs=(P("dp", "tensor"), P("dp", None)),
        check_vma=False,
    )
```

```python
import functools

import jax
import jax.numpy as jnp
from jax import lax
from jax.experimental import pallas as pl
from jax.experimental.pallas import tpu as pltpu
from jax.sharding import PartitionSpec as P

EPS = 1e-05
MESH = pl.DeviceIdType.MESH
F32 = jnp.float32
BF16 = jnp.bfloat16

L = 256
D = 768
SLAB = 384
N_Y = 4
N_Z = 8
N_X = 4
ROWS = 512


def split3(values):
    high = values.astype(BF16)
    rest = values - high.astype(F32)
    mid = rest.astype(BF16)
    low = (rest - mid.astype(F32)).astype(BF16)
    return high, mid, low


def pick(hot, values):
    parts = split3(values)
    return sum(jnp.dot(hot, part, preferred_element_type=F32) for part in parts)


class Ring:
    def __init__(self, sems, n, me, right, left, parts):
        self.n, self.me, self.right, self.left = n, me, right, left
        self.parts = parts
        self.sems = sems
        self.ids = [[(sems.take(), sems.take()) for _ in range(2)] for _ in range(n // 2)]

    def _at(self, offset):
        return lax.rem(self.me + offset + self.n, self.n)

    def start(self, step, part):
        a, b = self.ids[step - 1][part]
        last = step == self.n // 2
        if not last or part == 0:
            self.sems.send(self.parts(self._at(1 - step))[part], a, self.right)
        if not last or part == 1:
            self.sems.send(self.parts(self._at(step - 1))[part], b, self.left)

    def wait(self, step, part):
        a, b = self.ids[step - 1][part]
        last = step == self.n // 2
        if not last or part == 0:
            self.sems.arrived(self.parts(self._at(-step))[part], a, self.right)
        if not last or part == 1:
            self.sems.arrived(self.parts(self._at(step))[part], b, self.left)

    def begin(self):
        for part in range(2):
            self.start(1, part)

    def advance(self, step):
        for part in range(2):
            self.wait(step, part)
            if step < self.n // 2:
                self.start(step + 1, part)


class Direct:
    def __init__(self, sems, n, me, device, block):
        self.sems, self.n, self.me, self.device, self.block = sems, n, me, device, block
        self.numbers = [sems.take() for _ in range(n)]

    def begin(self):
        offsets = sorted(range(1, self.n), key=lambda k: -min(k, self.n - k))
        for k in offsets:
            i = lax.rem(self.me + k, self.n)
            self.sems.send(self.block(self.me), self.numbers[k], self.device(i))

    def done(self):
        for k in range(1, self.n):
            i = lax.rem(self.me + self.n - k, self.n)
            self.sems.arrived(self.block(i), self.numbers[k], self.device(i))


class Copies:
    def __init__(self, send, recv):
        self.send_sems, self.recv_sems = send, recv
        self.count = 0
        self.started = []

    def take(self):
        self.count += 1
        return self.count - 1

    def _copy(self, src, dst, number, device):
        return pltpu.make_async_remote_copy(
            src_ref=src,
            dst_ref=dst,
            send_sem=self.send_sems.at[number],
            recv_sem=self.recv_sems.at[number],
            device_id=device,
            device_id_type=MESH,
        )

    def send(self, src, number, device, dst=None):
        copy = self._copy(src, src if dst is None else dst, number, device)
        copy.start()
        self.started.append((None, copy.wait_send))

    def send_if(self, condition, src, number, device):
        @pl.when(condition)
        def _():
            self._copy(src, src, number, device).start()

        self.started.append(
            (condition, lambda: self._copy(src, src, number, device).wait_send())
        )

    def arrived(self, ref, number, device):
        self._copy(ref, ref, number, device).wait_recv()

    def finish(self):
        for condition, wait in self.started:
            if condition is None:
                wait()
            else:
                pl.when(condition)(wait)
        self.started = []


N_COPIES = 288


class Spread(Ring):
    def __init__(self, sems, n, me, right, left, sibling, mine, theirs):
        super().__init__(sems, n, me, right, left, mine)
        self.sibling, self.theirs = sibling, theirs
        self.hands = [(sems.take(), sems.take()) for _ in range(n)]

    def _hand(self, offset, part):
        number = self.hands[offset % self.n][part]
        self.sems.send(self.parts(self._at(offset))[part], number, self.sibling)

    def begin_part(self, part):
        self.start(1, part)
        self._hand(0, part)

    def begin(self):
        for part in range(2):
            self.begin_part(part)

    def advance(self, step):
        for part in range(2):
            self.wait(step, part)
            if step < self.n // 2:
                self.start(step + 1, part)
                self._hand(-step, part)
            self._hand(step, part)

    def done(self):
        for offset in range(self.n):
            for part in range(2):
                i = self._at(offset)
                self.sems.arrived(self.theirs(i)[part], self.hands[offset][part], self.sibling)


class Third:
    def __init__(self, sems, buf, x, y, core, at_x, at_y, y_rows, sibling):
        self.sems, self.buf, self.core, self.at_x, self.sibling = sems, buf, core, at_x, sibling
        self.x, self.tile = x, jnp.minimum(x, 2)
        self.along_y = Direct(
            sems, N_Y, y, at_y, lambda i: buf.at[core, self.tile, y_rows(i)]
        )
        self.numbers = [sems.take() for _ in range(N_X)]
        self.hands = [sems.take() for _ in range(N_X)]
        self.origins = [lax.rem(x + N_X - k, N_X) for k in range(N_X)]
        self.comes = [
            (i < 3) & jnp.logical_not((x == 3) & (i == 2)) for i in self.origins
        ]

    def begin_x(self):
        self.along_y.done()
        mine = self.buf.at[self.core, self.tile]
        for k in range(1, N_X):
            goes = self.x < 3
            if k == 1:
                goes = self.x < 2
            self.sems.send_if(goes, mine, self.numbers[k], self.at_x(lax.rem(self.x + k, N_X)))
        self.sems.send(mine, self.hands[0], self.sibling)

    def done_x(self):
        for k in range(1, N_X):
            ref = self.buf.at[self.core, jnp.minimum(self.origins[k], 2)]

            @pl.when(self.comes[k])
            def _():
                self.sems.arrived(ref, self.numbers[k], self.at_x(self.origins[k]))

            self.sems.send_if(self.comes[k], ref, self.hands[k], self.sibling)

    def done(self):
        self.sems.arrived(self.buf.at[1 - self.core, self.tile], self.hands[0], self.sibling)
        for k in range(1, N_X):
            ref = self.buf.at[1 - self.core, jnp.minimum(self.origins[k], 2)]

            @pl.when(self.comes[k])
            def _():
                self.sems.arrived(ref, self.hands[k], self.sibling)


def encode_kernel(
    lens_any,
    owner_any,
    list_any,
    weight_any,
    gain_one_any,
    shift_one_any,
    gain_two_any,
    shift_two_any,
    x_any,
    old_ref,
    wqkv_ref,
    wout_ref,
    wup_ref,
    wdown_ref,
    rot_ref,
    emb_out,
    ids_out,
    rows_out,
    rot_out,
    w_a,
    w_u,
    w_d,
    w_k,
    w_o,
    z_a,
    y_u,
    z_d,
    turned,
    lens_ref,
    owner_ref,
    list_ref,
    weight_ref,
    gain_one_ref,
    shift_one_ref,
    gain_two_ref,
    shift_two_ref,
    x_ref,
    rot_buf,
    old_buf,
    rot_send,
    mine_rows,
    owner_rows,
    emb_group,
    qkv,
    ctx,
    first,
    act,
    acc,
    send_sems,
    recv_sems,
    local_sems,
):
    dp = lax.axis_index("dp")
    tens = lax.axis_index("tensor")
    y, z = dp // N_Z, lax.rem(dp, N_Z)
    x, core = tens // 2, lax.rem(tens, 2)

    def at_y(i):
        return (i * N_Z + z, tens)

    def at_z(i):
        return (y * N_Z + i, tens)

    def at_x(i):
        return (dp, 2 * i + core)

    y_right, y_left = at_y(lax.rem(y + 1, N_Y)), at_y(lax.rem(y + N_Y - 1, N_Y))
    z_right, z_left = at_z(lax.rem(z + 1, N_Z)), at_z(lax.rem(z + N_Z - 1, N_Z))
    peers = [(dp, lax.rem(tens + k, 8)) for k in range(1, 8)]
    sibling = (dp, 2 * x + 1 - core)
    is_turn_self = tens == z
    turn = [(i * N_Z + tens, z) for i in range(N_Y)]

    third = jnp.minimum(x, 2)

    def cut(ref, at, tile=None):
        if tile is None:
            return ref.at[:, pl.ds(pl.multiple_of(at * SLAB, 128), SLAB)]
        return ref.at[:, pl.ds(pl.multiple_of(at * SLAB + tile * 128, 128), 128)]

    loads = [
        (cut(wqkv_ref, core), z_a.at[z, :, pl.ds(0, SLAB)]),
        (cut(wqkv_ref, 4 + core), z_a.at[z, :, pl.ds(SLAB, SLAB)]),
        (cut(wqkv_ref, 2 + core, third), z_a.at[z, :, pl.ds(2 * SLAB, 128)]),
        (wup_ref, y_u.at[y, x]),
        (wdown_ref, z_d.at[z, :, pl.ds(0, SLAB)]),
        (cut(wout_ref, core, third), z_d.at[z, :, pl.ds(SLAB, 128)]),
        (owner_any, owner_ref),
        (list_any, list_ref),
        (lens_any, lens_ref),
        (x_any, x_ref),
        (gain_one_any, gain_one_ref),
        (shift_one_any, shift_one_ref),
        (gain_two_any, gain_two_ref),
        (shift_two_any, shift_two_ref),
        (weight_any, weight_ref),
        (rot_ref, rot_buf),
        (old_ref, old_buf),
    ]
    loads = [
        pltpu.make_async_copy(src, dst, local_sems.at[i]) for i, (src, dst) in enumerate(loads)
    ]
    for load in loads:
        load.start()

    barrier = pltpu.get_barrier_semaphore()
    others = [at_y(lax.rem(y + k, N_Y)) for k in range(1, N_Y)]
    others += [at_z(lax.rem(z + k, N_Z)) for k in range(1, N_Z)]
    for device in others + peers:
        pl.semaphore_signal(barrier, inc=1, device_id=device, device_id_type=MESH)
    for i in range(N_Y):
        @pl.when(jnp.logical_not(jnp.logical_and(is_turn_self, y == i)))
        def _():
            pl.semaphore_signal(barrier, inc=1, device_id=turn[i], device_id_type=MESH)

    for load in loads[:6]:
        load.wait()
    pl.semaphore_wait(barrier, 17 + N_Y - is_turn_self.astype(jnp.int32))

    sems = Copies(send_sems, recv_sems)

    def z_rows(i):
        return pl.ds(pl.multiple_of(i * 96, 32), 96)

    def y_rows(i):
        return pl.ds(pl.multiple_of(i * 192, 64), 192)

    def y_last(buf, count):
        half = count // 2

        def parts(c, i):
            return [buf.at[pl.ds(c * count + k, half), y_rows(i)] for k in (0, half)]

        return Spread(
            sems, N_Y, y, y_right, y_left, sibling,
            lambda i: parts(core, i), lambda i: parts(1 - core, i),
        )

    def z_last(buf, count):
        half = count // 2

        def parts(c, i):
            return [buf.at[pl.ds(c * count + k, half), z_rows(i)] for k in (0, half)]

        return Spread(
            sems, N_Z, z, z_right, z_left, sibling,
            lambda i: parts(core, i), lambda i: parts(1 - core, i),
        )

    def assemble(blocks, full):
        wide = full.shape[-1]
        for i, block in enumerate(blocks):
            turned[i * 24 : (i + 1) * 24, 0:wide] = block.astype(F32)
        full[...] = turned[0 : 24 * len(blocks), 0:wide].astype(BF16)

    az = Direct(sems, N_Z, z, at_z, lambda i: z_a.at[i])
    dz = Direct(sems, N_Z, z, at_z, lambda i: z_d.at[i])
    ux = Direct(sems, N_X, x, at_x, lambda i: y_u.at[y, i])
    uy = Direct(sems, N_Y, y, at_y, lambda i: y_u.at[i])
    dx = Direct(sems, N_X, x, at_x, lambda i: w_d.at[core * 4 + i, y_rows(y)])
    iz = Direct(sems, N_Z, z, at_z, lambda i: ids_out.at[y, i])
    iy = Direct(sems, N_Y, y, at_y, lambda i: ids_out.at[i])
    qv, u_z, d_y = y_last(w_a, 2), z_last(w_u, 4), y_last(w_d, 4)
    k_x = Third(sems, w_k, x, y, core, at_x, at_y, y_rows, sibling)
    o_x = Third(sems, w_o, x, y, core, at_x, at_y, y_rows, sibling)

    az.begin()
    ux.begin()
    dz.begin()
    for load in loads[6:8]:
        load.wait()
    ids_rows = [
        jnp.full((1, 128), owner_ref[i] * 1024 + list_ref[i], jnp.int32) for i in range(16)
    ]
    ids_out[y, z] = jnp.concatenate(ids_rows, axis=0).astype(F32)
    iz.begin()
    ux.done()
    uy.begin()
    az.done()
    assemble(
        [z_a[i, :, 2 * SLAB : 2 * SLAB + 128] for i in range(N_Z)],
        w_k.at[core, third, y_rows(y)],
    )
    k_x.along_y.begin()
    for s in range(2):
        assemble(
            [z_a[i, :, s * SLAB : (s + 1) * SLAB] for i in range(N_Z)],
            w_a.at[core * 2 + s, y_rows(y)],
        )
        qv.begin_part(s)
    uy.done()
    for s in range(4):
        assemble([y_u[i, s] for i in range(N_Y)], w_u.at[core * 4 + s, z_rows(z)])
    u_z.begin()
    k_x.begin_x()
    dz.done()
    assemble([z_d[i, :, 0:SLAB] for i in range(N_Z)], w_d.at[core * 4 + x, y_rows(y)])
    dx.begin()
    assemble(
        [z_d[i, :, SLAB : SLAB + 128] for i in range(N_Z)], w_o.at[core, third, y_rows(y)]
    )
    iz.done()
    iy.begin()

    for load in loads[8:]:
        load.wait()
    column = lax.broadcasted_iota(jnp.int32, (1, D), 1)
    by_z = column // 96
    by_y = (column - by_z * 96) // 24
    source = by_y * 192 + by_z * 24 + (column - by_z * 96 - by_y * 24)
    order = lax.broadcasted_iota(jnp.int32, (D, D), 0) == source
    order = order.astype(F32).astype(BF16)
    for k in range(8):
        rot_send[k] = rot_buf[:, k * 96 : (k + 1) * 96]
    qv.advance(1)
    o_x.along_y.begin()
    u_z.advance(1)
    iy.done()

    n_slots = 8
    wanted = jnp.concatenate([ids_out[i, tens] for i in range(N_Y)], axis=0)
    owners = jnp.floor(wanted * (1.0 / 1024))
    lists = wanted - owners * 1024.0
    own = (owners == dp.astype(F32)).astype(F32)
    one = lax.broadcasted_iota(jnp.int32, (64, 64), 0)
    two = lax.broadcasted_iota(jnp.int32, (64, 64), 1)
    earlier = ((one > two) & (one // 16 == two // 16)).astype(BF16)
    rank = jnp.dot(earlier, own.astype(BF16), preferred_element_type=F32)
    hots = []
    for r in range(2):
        named = jnp.where((own > 0.5) & (rank == float(r)), lists + 1.0, 0.0)
        named = jnp.sum(named.reshape(N_Y, 16, 128), axis=1) - 1.0
        hots.append(named)
    named = jnp.concatenate(hots, axis=0)
    places = lax.broadcasted_iota(jnp.int32, (n_slots, 1024), 1).astype(F32)
    hot = places == named[:, 0:1]
    mine_rows[:, 0:D] = pick(hot.astype(F32).astype(BF16), old_buf[...])
    mine_rows[:, D : D + 128] = jnp.broadcast_to(
        jnp.sum(
            jnp.where(hot, weight_ref[...].astype(F32).reshape(1, 1024), 0.0),
            axis=1,
            keepdims=True,
        ),
        (n_slots, 128),
    )
    qv.advance(2)
    k_x.done_x()
    dx.done()
    d_y.begin()
    o_x.begin_x()
    qv.done()
    k_x.done()

    turn_numbers = [sems.take() for _ in range(N_Y)]
    turn_to = [((lax.rem(y + k, N_Y)) * N_Z + tens, z) for k in range(N_Y)]
    rot_numbers = [sems.take() for _ in range(7)]
    row_numbers = [sems.take() for _ in range(7)]
    rot_place = pl.ds(pl.multiple_of(tens * 96, 32), 96)

    def send_rows_and_rotation():
        for k in range(1, N_Y):
            sems.send(mine_rows, turn_numbers[k], turn_to[k], dst=owner_rows.at[y])

        @pl.when(jnp.logical_not(is_turn_self))
        def _():
            copy = sems._copy(mine_rows, owner_rows.at[y], turn_numbers[0], turn_to[0])
            copy.start()
            copy.wait_send()

        @pl.when(is_turn_self)
        def _():
            owner_rows[y] = mine_rows[...]

        rot_out[rot_place, :] = rot_send[tens]
        for k in range(1, 8):
            other = lax.rem(tens + k, 8)
            sems.send(
                rot_send.at[other], rot_numbers[k - 1], peers[k - 1], dst=rot_out.at[rot_place]
            )

    def share_rows():
        @pl.when(jnp.logical_not(is_turn_self))
        def _():
            sems.arrived(owner_rows.at[y], turn_numbers[0], turn_to[0])

        for k in range(1, N_Y):
            sems.arrived(
                owner_rows.at[lax.rem(y + N_Y - k, N_Y)], turn_numbers[k], turn_to[k]
            )
        for r in range(2):
            for i in range(N_Y):
                rows_out[tens, r * N_Y + i : r * N_Y + i + 1, :] = owner_rows[
                    i, pl.ds(r * N_Y + y, 1), :
                ]
        for k in range(1, 8):
            sems.send(rows_out.at[tens], row_numbers[k - 1], peers[k - 1])

    def project(c):
        for at in range(2):
            part = jnp.dot(x_ref[...], w_a[c * 2 + at], preferred_element_type=F32).astype(BF16)
            if at == 0:
                part = part * 0.125
            qkv[c * 3 + at] = part
        for j in range(3):
            part = jnp.dot(x_ref[...], w_k[c, j], preferred_element_type=F32).astype(BF16)
            qkv[c * 3 + 2, :, j * 128 : (j + 1) * 128] = part

    lane = lax.broadcasted_iota(jnp.int32, (1, 128), 1)
    low = (lane < 64).astype(F32).astype(BF16)
    both_halves = (low, 1 - low)
    key_at = lax.broadcasted_iota(jnp.int32, (1, L), 1)

    def attend(p, c, j):
        keys_ok = key_at < lens_ref[2 * tens + p]
        tokens = slice(p * L, (p + 1) * L)
        columns = slice(j * 128, (j + 1) * 128)
        q = qkv[c * 3, tokens, columns]
        v = qkv[c * 3 + 1, tokens, columns]
        k = qkv[c * 3 + 2, tokens, columns]
        total = None
        for half in both_halves:
            scores = lax.dot_general(
                q * half, k, (((1,), (1,)), ((), ())), preferred_element_type=F32
            )
            scores = jnp.where(keys_ok, scores, -1e30)
            powers = jnp.exp(scores - jnp.max(scores, axis=1, keepdims=True))
            scale = 1.0 / jnp.sum(powers, axis=1, keepdims=True)
            probs = (powers * scale).astype(BF16)
            part = jnp.dot(probs, v * half, preferred_element_type=F32)
            total = part if total is None else total + part
        ctx[tokens, c * SLAB + j * 128 : c * SLAB + (j + 1) * 128] = total.astype(BF16)

    def mix(b):
        tokens = slice(b * L, (b + 1) * L)
        mixed = jnp.concatenate(
            [
                jnp.dot(ctx[tokens, :], w_o[c, j], preferred_element_type=F32)
                for c in range(2)
                for j in range(3)
            ],
            axis=1,
        )
        values = x_ref[tokens, :].astype(F32) + mixed
        centered = values - jnp.mean(values, axis=1, keepdims=True)
        spread = jnp.mean(centered * centered, axis=1, keepdims=True)
        normed = centered * lax.rsqrt(spread + EPS) * gain_one_ref[...].reshape(
            1, D
        ) + shift_one_ref[...].reshape(1, D)
        normed = normed.astype(BF16)
        acc[tokens, :] = normed.astype(F32)
        first[tokens, :] = jnp.dot(normed, order, preferred_element_type=F32).astype(BF16)

    u_z.advance(2)
    project(0)
    send_rows_and_rotation()
    project(1)
    steps = {
        1: lambda: u_z.advance(3),
        3: o_x.done_x,
        6: share_rows,
        8: lambda: u_z.advance(4),
        11: lambda: d_y.advance(1),
    }
    for n, (c, p, j) in enumerate(
        (c, p, j) for c in range(2) for p in range(2) for j in range(3)
    ):
        attend(p, c, j)
        if n in steps:
            steps[n]()
    o_x.done()
    mix(0)
    mix(1)
    u_z.done()

    def raise_slab(s, carry):
        for b in range(2):
            tokens = slice(b * L, (b + 1) * L)
            up = jnp.dot(first[tokens, :], w_u[s], preferred_element_type=F32)
            act[s, tokens, :] = (0.5 * up * (1.0 + lax.erf(up * (0.5**0.5)))).astype(BF16)
        return carry

    def lower_slab(s, carry):
        for b in range(2):
            tokens = slice(b * L, (b + 1) * L)
            acc[tokens, :] += lax.dot_general(
                act[s, tokens, :], w_d[s], (((1,), (1,)), ((), ())), preferred_element_type=F32
            )
        return carry

    lax.fori_loop(0, 8, raise_slab, 0)
    d_y.advance(2)
    d_y.done()
    lax.fori_loop(0, 8, lower_slab, 0)

    token_at = lax.broadcasted_iota(jnp.int32, (L, 1), 0)
    for p in range(2):
        length = lens_ref[2 * tens + p]
        values = acc[p * L : (p + 1) * L, :]
        centered = values - jnp.mean(values, axis=1, keepdims=True)
        spread = jnp.mean(centered * centered, axis=1, keepdims=True)
        scaled = centered * lax.rsqrt(spread + EPS)
        pooled = jnp.sum(jnp.where(token_at < length, scaled, 0.0), axis=0, keepdims=True)
        emb = pooled / length.astype(F32) * gain_two_ref[...].reshape(1, D)
        emb_group[tens, p : p + 1, :] = emb + shift_two_ref[...].reshape(1, D)

    group_numbers = [sems.take() for _ in range(7)]
    for k in range(1, 8):
        sems.send(emb_group.at[tens], group_numbers[k - 1], peers[k - 1])
    sems.finish()
    for k in range(1, 8):
        origin = lax.rem(tens + 8 - k, 8)
        place = pl.ds(pl.multiple_of(origin * 96, 32), 96)
        sems.arrived(rot_out.at[place], rot_numbers[k - 1], peers[k - 1])
        sems.arrived(rows_out.at[origin], row_numbers[k - 1], peers[k - 1])
    for k in range(1, 8):
        other = lax.rem(tens + 8 - k, 8)
        sems.arrived(emb_group.at[other], group_numbers[k - 1], peers[k - 1])
    for t in range(8):
        both = emb_group[t]
        @pl.when(core == 0)
        def _():
            emb_out[0, y, z, 2 * t : 2 * t + 2, :] = both[:, :SLAB]
        @pl.when(core == 1)
        def _():
            emb_out[1, y, z, 2 * t : 2 * t + 2, :] = both[:, SLAB:]
    ze = Direct(sems, N_Z, z, at_z, lambda i: emb_out.at[core, y, i])

    def emb_parts(c, i):
        return emb_out.at[c, i, pl.ds(0, 4)], emb_out.at[c, i, pl.ds(4, 4)]

    ye = Spread(
        sems, N_Y, y, y_right, y_left, sibling,
        lambda i: emb_parts(core, i), lambda i: emb_parts(1 - core, i),
    )
    ze.begin()
    ze.done()
    ye.begin()
    ye.advance(1)
    ye.advance(2)
    ye.done()
    sems.finish()


def finish_kernel(emb_ref, ids_ref, rows_ref, rot_ref, weight_ref, old_ref, rotated_ref, centroids_ref, slot_ids, slots):
    step = pl.program_id(0)
    dp = lax.axis_index("dp")

    @pl.when(step == 0)
    def _():
        ids_row = jnp.transpose(ids_ref[...])[0:8, :]
        ids = ids_ref[pl.ds(pl.multiple_of(dp * 16, 16), 16), :]
        owners = jnp.floor(ids * (1.0 / 1024))
        owner_y = jnp.floor(owners * (1.0 / N_Z))
        owner_z = owners - owner_y * N_Z
        one = lax.broadcasted_iota(jnp.int32, (16, 16), 0)
        two = lax.broadcasted_iota(jnp.int32, (16, 16), 1)
        owners_row = jnp.sum(jnp.where(one == two, owners[:, 0:16], 0.0), axis=0, keepdims=True)
        rank = jnp.sum(
            ((owners[:, 0:16] == owners_row) & (two < one)).astype(F32), axis=1, keepdims=True
        )
        place = owner_z * 8.0 + rank * N_Y + owner_y
        spots = lax.broadcasted_iota(jnp.int32, (16, 64), 1).astype(F32)
        hot = (place[:, 0:64] == spots).astype(F32).astype(BF16)
        old = pick(hot, rows_ref[...])
        same = ids[:, 0:1] == ids_row[0:1, :]
        counts = jnp.sum(same.astype(F32), axis=1, keepdims=True)
        mine = jnp.floor(ids_row * (1.0 / 1024)) == dp.astype(F32)
        before = lax.broadcasted_iota(jnp.int32, (ROWS, ROWS), 0) < lax.broadcasted_iota(
            jnp.int32, (ROWS, ROWS), 1
        )
        spot = jnp.dot(
            mine.astype(F32).astype(BF16),
            before.astype(F32).astype(BF16),
            preferred_element_type=F32,
        )
        numbers = lax.broadcasted_iota(jnp.int32, (64, ROWS), 0).astype(F32)
        placed = (numbers == spot[0:1, :]) & mine[0:1, :]
        named = jnp.sum(jnp.where(placed, ids_row[0:1, :] + 1.0, 0.0), axis=1, keepdims=True)
        named = jnp.concatenate([named - 1.0, jnp.full((64, 1), -1.0, F32)], axis=0)
        slot_ids[...] = jnp.transpose(jnp.broadcast_to(named, (128, 128)))[0:8, :]
        taken = jnp.concatenate([same.astype(F32), placed.astype(F32)], axis=0).astype(BF16)
        weight = old[:, D : D + 1]
        result = None
        for h in range(2):
            picked = pick(taken, emb_ref[h])
            sums = picked[0:16, :]
            for k, part in enumerate(split3(picked[16:80, :])):
                slots[k * 64 : (k + 1) * 64, h * SLAB : (h + 1) * SLAB] = part
            centroids = (weight * old[:, h * SLAB : (h + 1) * SLAB] + sums) / (weight + counts)
            resid = emb_ref[h, pl.ds(pl.multiple_of(dp * 16, 16), 16), :] - centroids
            part = jnp.dot(
                resid,
                rot_ref[h * SLAB : (h + 1) * SLAB, :],
                precision=lax.Precision.HIGHEST,
                preferred_element_type=F32,
            )
            result = part if result is None else result + part
        rotated_ref[...] = result

    one = lax.broadcasted_iota(jnp.int32, (128, 128), 0)
    two = lax.broadcasted_iota(jnp.int32, (128, 128), 1)
    weight = jnp.concatenate(
        [
            jnp.sum(
                jnp.where(one == two, weight_ref[pl.ds(step * 4 + i, 1), :], 0.0),
                axis=1,
                keepdims=True,
            )
            for i in range(4)
        ],
        axis=0,
    )
    number = lax.broadcasted_iota(jnp.int32, (512, 64), 0) + dp * 1024 + step * 512
    hot = (number.astype(F32) == slot_ids[0:1, 0:64]).astype(F32)
    counts = jnp.sum(hot, axis=1, keepdims=True)
    hot = jnp.concatenate([hot, hot, hot], axis=1).astype(BF16)
    for h in range(2):
        columns = slice(h * SLAB, (h + 1) * SLAB)
        sums = jnp.dot(hot, slots[:, columns], preferred_element_type=F32)
        centroids_ref[:, columns] = (weight * old_ref[:, columns] + sums) / (weight + counts)


VMEM = pl.BlockSpec(memory_space=pltpu.VMEM)
HBM = pl.BlockSpec(memory_space=pltpu.HBM)


def local(
    hidden,
    lengths,
    owner_of,
    list_local,
    old_weight,
    old_centroids,
    w_qkv,
    w_out,
    gain_one,
    shift_one,
    w_up,
    w_down,
    gain_two,
    shift_two,
    rotation,
):
    weight = old_weight.astype(F32)
    vmem = pltpu.VMEM
    emb, ids, rows, rot = pl.pallas_call(
        encode_kernel,
        out_shape=(
            jax.ShapeDtypeStruct((2, N_Y, N_Z, 16, SLAB), F32),
            jax.ShapeDtypeStruct((N_Y, N_Z, 16, 128), F32),
            jax.ShapeDtypeStruct((8, 8, D + 128), F32),
            jax.ShapeDtypeStruct((D, 96), F32),
        ),
        in_specs=[HBM] * 15,
        out_specs=(VMEM,) * 4,
        scratch_shapes=[
            vmem((4, D, SLAB), BF16),
            vmem((8, D, SLAB), BF16),
            vmem((8, D, SLAB), BF16),
            vmem((2, 3, D, 128), BF16),
            vmem((2, 3, D, 128), BF16),
            vmem((N_Z, 24, 2 * SLAB + 128), BF16),
            vmem((N_Y, 4, 24, SLAB), BF16),
            vmem((N_Z, 24, SLAB + 128), BF16),
            vmem((192, SLAB), F32),
            pltpu.SMEM((16,), jnp.int32),
            pltpu.SMEM((16,), jnp.int32),
            pltpu.SMEM((16,), jnp.int32),
            vmem((1024,), jnp.int32),
            vmem((D,), F32),
            vmem((D,), F32),
            vmem((D,), F32),
            vmem((D,), F32),
            vmem((ROWS, D), BF16),
            vmem((96, D), F32),
            vmem((1024, D), F32),
            vmem((8, 96, 96), F32),
            vmem((8, D + 128), F32),
            vmem((N_Y, 8, D + 128), F32),
            vmem((8, 2, D), F32),
            vmem((6, ROWS, SLAB), BF16),
            vmem((ROWS, D), BF16),
            vmem((ROWS, D), BF16),
            vmem((8, ROWS, SLAB), BF16),
            vmem((ROWS, D), F32),
            pltpu.SemaphoreType.DMA((N_COPIES,)),
            pltpu.SemaphoreType.DMA((N_COPIES,)),
            pltpu.SemaphoreType.DMA((17,)),
        ],
        compiler_params=pltpu.CompilerParams(
            collective_id=0, has_side_effects=True, vmem_limit_bytes=60 * 2**20
        ),
    )(
        lengths,
        owner_of.reshape(16),
        list_local,
        old_weight,
        gain_one,
        shift_one,
        gain_two,
        shift_two,
        hidden.reshape(ROWS, D),
        old_centroids,
        w_qkv,
        w_out,
        w_up,
        w_down.T,
        rotation,
    )
    whole = lambda *shape: pl.BlockSpec(shape, lambda i: (0,) * len(shape))
    return pl.pallas_call(
        finish_kernel,
        grid=(2,),
        out_shape=(
            jax.ShapeDtypeStruct((16, 96), F32),
            jax.ShapeDtypeStruct((1024, D), F32),
        ),
        in_specs=[
            whole(2, ROWS, SLAB),
            whole(ROWS, 128),
            whole(64, D + 128),
            whole(D, 96),
            whole(8, 128),
            pl.BlockSpec((512, D), lambda i: (i, 0)),
        ],
        out_specs=(whole(16, 96), pl.BlockSpec((512, D), lambda i: (i, 0))),
        scratch_shapes=[vmem((8, 128), F32), vmem((192, D), BF16)],
        compiler_params=pltpu.CompilerParams(vmem_limit_bytes=60 * 2**20),
    )(
        emb.reshape(2, ROWS, SLAB),
        ids.reshape(ROWS, 128),
        rows.reshape(64, D + 128),
        rot,
        weight.reshape(8, 128),
        old_centroids,
    )


def solution(mesh):
    return jax.shard_map(
        local,
        mesh=mesh,
        in_specs=(
            P(("dp", "tensor"), None, None),
            P("dp"),
            P("dp", None),
            P("dp"),
            P("dp"),
            P("dp", None),
            P("dp", None),
            P("dp", None),
            P(),
            P(),
            P("dp", "tensor"),
            P("tensor", "dp"),
            P(),
            P(),
            P("tensor", None),
        ),
        out_specs=(P("dp", "tensor"), P("dp", None)),
        check_vma=False,
    )
```

```python
import functools

import jax
import jax.numpy as jnp
from jax import lax
from jax.experimental import pallas as pl
from jax.experimental.pallas import tpu as pltpu
from jax.sharding import PartitionSpec as P

EPS = 1e-05
MESH = pl.DeviceIdType.MESH
F32 = jnp.float32
BF16 = jnp.bfloat16

L = 256
D = 768
SLAB = 384
N_Y = 4
N_Z = 8
N_X = 4
ROWS = 512


def split3(values):
    high = values.astype(BF16)
    rest = values - high.astype(F32)
    mid = rest.astype(BF16)
    low = (rest - mid.astype(F32)).astype(BF16)
    return high, mid, low


def pick(hot, values):
    parts = split3(values)
    return sum(jnp.dot(hot, part, preferred_element_type=F32) for part in parts)


class Ring:
    def __init__(self, sems, n, me, right, left, parts):
        self.n, self.me, self.right, self.left = n, me, right, left
        self.parts = parts
        self.sems = sems
        self.ids = [[(sems.take(), sems.take()) for _ in range(2)] for _ in range(n // 2)]

    def _at(self, offset):
        return lax.rem(self.me + offset + self.n, self.n)

    def start(self, step, part):
        a, b = self.ids[step - 1][part]
        last = step == self.n // 2
        if not last or part == 0:
            self.sems.send(self.parts(self._at(1 - step))[part], a, self.right)
        if not last or part == 1:
            self.sems.send(self.parts(self._at(step - 1))[part], b, self.left)

    def wait(self, step, part):
        a, b = self.ids[step - 1][part]
        last = step == self.n // 2
        if not last or part == 0:
            self.sems.arrived(self.parts(self._at(-step))[part], a, self.right)
        if not last or part == 1:
            self.sems.arrived(self.parts(self._at(step))[part], b, self.left)

    def begin(self):
        for part in range(2):
            self.start(1, part)

    def advance(self, step):
        for part in range(2):
            self.wait(step, part)
            if step < self.n // 2:
                self.start(step + 1, part)


class Direct:
    def __init__(self, sems, n, me, device, block):
        self.sems, self.n, self.me, self.device, self.block = sems, n, me, device, block
        self.numbers = [sems.take() for _ in range(n)]

    def begin(self):
        offsets = sorted(range(1, self.n), key=lambda k: -min(k, self.n - k))
        for k in offsets:
            i = lax.rem(self.me + k, self.n)
            self.sems.send(self.block(self.me), self.numbers[k], self.device(i))

    def done(self):
        for k in range(1, self.n):
            i = lax.rem(self.me + self.n - k, self.n)
            self.sems.arrived(self.block(i), self.numbers[k], self.device(i))


class Copies:
    def __init__(self, send, recv):
        self.send_sems, self.recv_sems = send, recv
        self.count = 0
        self.started = []

    def take(self):
        self.count += 1
        return self.count - 1

    def _copy(self, src, dst, number, device):
        return pltpu.make_async_remote_copy(
            src_ref=src,
            dst_ref=dst,
            send_sem=self.send_sems.at[number],
            recv_sem=self.recv_sems.at[number],
            device_id=device,
            device_id_type=MESH,
        )

    def send(self, src, number, device, dst=None):
        copy = self._copy(src, src if dst is None else dst, number, device)
        copy.start()
        self.started.append((None, copy.wait_send))

    def send_if(self, condition, src, number, device):
        @pl.when(condition)
        def _():
            self._copy(src, src, number, device).start()

        self.started.append(
            (condition, lambda: self._copy(src, src, number, device).wait_send())
        )

    def arrived(self, ref, number, device):
        self._copy(ref, ref, number, device).wait_recv()

    def finish(self):
        for condition, wait in self.started:
            if condition is None:
                wait()
            else:
                pl.when(condition)(wait)
        self.started = []


N_COPIES = 288


class Spread(Ring):
    def __init__(self, sems, n, me, right, left, sibling, mine, theirs):
        super().__init__(sems, n, me, right, left, mine)
        self.sibling, self.theirs = sibling, theirs
        self.hands = [(sems.take(), sems.take()) for _ in range(n)]

    def _hand(self, offset, part):
        number = self.hands[offset % self.n][part]
        self.sems.send(self.parts(self._at(offset))[part], number, self.sibling)

    def begin_part(self, part):
        self.start(1, part)
        self._hand(0, part)

    def begin(self):
        for part in range(2):
            self.begin_part(part)

    def advance(self, step):
        for part in range(2):
            self.wait(step, part)
            if step < self.n // 2:
                self.start(step + 1, part)
                self._hand(-step, part)
            self._hand(step, part)

    def done(self, offsets=None):
        for offset in range(self.n) if offsets is None else offsets:
            for part in range(2):
                i = self._at(offset)
                self.sems.arrived(self.theirs(i)[part], self.hands[offset][part], self.sibling)


class Third:
    def __init__(self, sems, buf, x, y, core, at_x, at_y, y_rows, sibling):
        self.sems, self.buf, self.core, self.at_x, self.sibling = sems, buf, core, at_x, sibling
        self.x, self.tile = x, jnp.minimum(x, 2)
        self.along_y = Direct(
            sems, N_Y, y, at_y, lambda i: buf.at[core, self.tile, y_rows(i)]
        )
        self.numbers = [sems.take() for _ in range(N_X)]
        self.hands = [sems.take() for _ in range(N_X)]
        self.origins = [lax.rem(x + N_X - k, N_X) for k in range(N_X)]
        self.comes = [
            (i < 3) & jnp.logical_not((x == 3) & (i == 2)) for i in self.origins
        ]

    def begin_x(self):
        self.along_y.done()
        mine = self.buf.at[self.core, self.tile]
        for k in range(1, N_X):
            goes = self.x < 3
            if k == 1:
                goes = self.x < 2
            self.sems.send_if(goes, mine, self.numbers[k], self.at_x(lax.rem(self.x + k, N_X)))
        self.sems.send(mine, self.hands[0], self.sibling)

    def done_x(self):
        for k in range(1, N_X):
            ref = self.buf.at[self.core, jnp.minimum(self.origins[k], 2)]

            @pl.when(self.comes[k])
            def _():
                self.sems.arrived(ref, self.numbers[k], self.at_x(self.origins[k]))

            self.sems.send_if(self.comes[k], ref, self.hands[k], self.sibling)

    def done(self):
        self.sems.arrived(self.buf.at[1 - self.core, self.tile], self.hands[0], self.sibling)
        for k in range(1, N_X):
            ref = self.buf.at[1 - self.core, jnp.minimum(self.origins[k], 2)]

            @pl.when(self.comes[k])
            def _():
                self.sems.arrived(ref, self.hands[k], self.sibling)


def encode_kernel(
    lens_any,
    owner_any,
    list_any,
    weight_any,
    gain_one_any,
    shift_one_any,
    gain_two_any,
    shift_two_any,
    x_any,
    old_ref,
    wqkv_ref,
    wout_ref,
    wup_ref,
    wdown_ref,
    rot_ref,
    emb_out,
    ids_out,
    rows_out,
    rot_out,
    w_a,
    w_u,
    w_d,
    w_e,
    w_k,
    w_o,
    z_a,
    y_u,
    z_d,
    turned,
    lens_ref,
    owner_ref,
    list_ref,
    weight_ref,
    gain_one_ref,
    shift_one_ref,
    gain_two_ref,
    shift_two_ref,
    x_ref,
    rot_buf,
    old_buf,
    rot_send,
    mine_rows,
    owner_rows,
    emb_group,
    qkv,
    ctx,
    first,
    act,
    acc,
    send_sems,
    recv_sems,
    local_sems,
):
    dp = lax.axis_index("dp")
    tens = lax.axis_index("tensor")
    y, z = dp // N_Z, lax.rem(dp, N_Z)
    x, core = tens // 2, lax.rem(tens, 2)

    def at_y(i):
        return (i * N_Z + z, tens)

    def at_z(i):
        return (y * N_Z + i, tens)

    def at_x(i):
        return (dp, 2 * i + core)

    y_right, y_left = at_y(lax.rem(y + 1, N_Y)), at_y(lax.rem(y + N_Y - 1, N_Y))
    z_right, z_left = at_z(lax.rem(z + 1, N_Z)), at_z(lax.rem(z + N_Z - 1, N_Z))
    peers = [(dp, lax.rem(tens + k, 8)) for k in range(1, 8)]
    sibling = (dp, 2 * x + 1 - core)
    is_turn_self = tens == z
    turn = [(i * N_Z + tens, z) for i in range(N_Y)]

    third = jnp.minimum(x, 2)

    def cut(ref, at, tile=None):
        if tile is None:
            return ref.at[:, pl.ds(pl.multiple_of(at * SLAB, 128), SLAB)]
        return ref.at[:, pl.ds(pl.multiple_of(at * SLAB + tile * 128, 128), 128)]

    loads = [
        (cut(wqkv_ref, core), z_a.at[z, :, pl.ds(0, SLAB)]),
        (cut(wqkv_ref, 4 + core), z_a.at[z, :, pl.ds(SLAB, SLAB)]),
        (cut(wqkv_ref, 2 + core, third), z_a.at[z, :, pl.ds(2 * SLAB, 128)]),
        (wup_ref, y_u.at[y, x]),
        (wdown_ref, z_d.at[z, :, pl.ds(0, SLAB)]),
        (cut(wout_ref, core, third), z_d.at[z, :, pl.ds(SLAB, 128)]),
        (owner_any, owner_ref),
        (list_any, list_ref),
        (lens_any, lens_ref),
        (x_any, x_ref),
        (gain_one_any, gain_one_ref),
        (shift_one_any, shift_one_ref),
        (gain_two_any, gain_two_ref),
        (shift_two_any, shift_two_ref),
        (weight_any, weight_ref),
        (rot_ref, rot_buf),
        (old_ref, old_buf),
    ]
    loads = [
        pltpu.make_async_copy(src, dst, local_sems.at[i]) for i, (src, dst) in enumerate(loads)
    ]
    for load in loads:
        load.start()

    barrier = pltpu.get_barrier_semaphore()
    others = [at_y(lax.rem(y + k, N_Y)) for k in range(1, N_Y)]
    others += [at_z(lax.rem(z + k, N_Z)) for k in range(1, N_Z)]
    for device in others + peers:
        pl.semaphore_signal(barrier, inc=1, device_id=device, device_id_type=MESH)
    for i in range(N_Y):
        @pl.when(jnp.logical_not(jnp.logical_and(is_turn_self, y == i)))
        def _():
            pl.semaphore_signal(barrier, inc=1, device_id=turn[i], device_id_type=MESH)

    for load in loads[:6]:
        load.wait()
    pl.semaphore_wait(barrier, 17 + N_Y - is_turn_self.astype(jnp.int32))

    sems = Copies(send_sems, recv_sems)

    def z_rows(i):
        return pl.ds(pl.multiple_of(i * 96, 32), 96)

    def y_rows(i):
        return pl.ds(pl.multiple_of(i * 192, 64), 192)

    def y_last(buf, count):
        half = count // 2

        def parts(c, i):
            return [buf.at[pl.ds(c * count + k, half), y_rows(i)] for k in (0, half)]

        return Spread(
            sems, N_Y, y, y_right, y_left, sibling,
            lambda i: parts(core, i), lambda i: parts(1 - core, i),
        )

    def z_last(buf, count):
        half = count // 2

        def parts(c, i):
            return [buf.at[pl.ds(c * count + k, half), z_rows(i)] for k in (0, half)]

        return Spread(
            sems, N_Z, z, z_right, z_left, sibling,
            lambda i: parts(core, i), lambda i: parts(1 - core, i),
        )

    def assemble(blocks, full):
        wide = full.shape[-1]
        for i, block in enumerate(blocks):
            turned[i * 24 : (i + 1) * 24, 0:wide] = block.astype(F32)
        full[...] = turned[0 : 24 * len(blocks), 0:wide].astype(BF16)

    az = Direct(sems, N_Z, z, at_z, lambda i: z_a.at[i])
    dz = Direct(sems, N_Z, z, at_z, lambda i: z_d.at[i])
    ux = Direct(sems, N_X, x, at_x, lambda i: y_u.at[y, i])
    uy = Direct(sems, N_Y, y, at_y, lambda i: y_u.at[i])
    dx = Direct(sems, N_X, x, at_x, lambda i: w_d.at[core * 4 + i, y_rows(y)])
    ey = Direct(sems, N_Y, y, at_y, lambda i: w_e.at[core * 4 + x, y_rows(i)])
    ex = Direct(sems, N_X, x, at_x, lambda i: w_e.at[core * 4 + i])
    e_hand = sems.take()
    iz = Direct(sems, N_Z, z, at_z, lambda i: ids_out.at[y, i])
    iy = Direct(sems, N_Y, y, at_y, lambda i: ids_out.at[i])
    qv, u_z, d_y = y_last(w_a, 2), z_last(w_u, 4), y_last(w_d, 4)
    k_x = Third(sems, w_k, x, y, core, at_x, at_y, y_rows, sibling)
    o_x = Third(sems, w_o, x, y, core, at_x, at_y, y_rows, sibling)

    az.begin()
    ux.begin()
    dz.begin()
    for load in loads[6:8]:
        load.wait()
    ids_rows = [
        jnp.full((1, 128), owner_ref[i] * 1024 + list_ref[i], jnp.int32) for i in range(16)
    ]
    ids_out[y, z] = jnp.concatenate(ids_rows, axis=0).astype(F32)
    iz.begin()
    ux.done()
    uy.begin()
    az.done()
    assemble(
        [z_a[i, :, 2 * SLAB : 2 * SLAB + 128] for i in range(N_Z)],
        w_k.at[core, third, y_rows(y)],
    )
    k_x.along_y.begin()
    for s in range(2):
        assemble(
            [z_a[i, :, s * SLAB : (s + 1) * SLAB] for i in range(N_Z)],
            w_a.at[core * 2 + s, y_rows(y)],
        )
        qv.begin_part(s)
    uy.done()
    for s in range(4):
        assemble([y_u[i, s] for i in range(N_Y)], w_u.at[core * 4 + s, z_rows(z)])
    u_z.begin()
    k_x.begin_x()
    dz.done()
    assemble([z_d[i, :, 0:256] for i in range(N_Z)], w_d.at[core * 4 + x, y_rows(y)])
    dx.begin()
    assemble([z_d[i, :, 256:SLAB] for i in range(N_Z)], w_e.at[core * 4 + x, y_rows(y)])
    assemble(
        [z_d[i, :, SLAB : SLAB + 128] for i in range(N_Z)], w_o.at[core, third, y_rows(y)]
    )
    iz.done()
    iy.begin()

    for load in loads[8:]:
        load.wait()
    column = lax.broadcasted_iota(jnp.int32, (1, D), 1)
    by_z = column // 96
    by_y = (column - by_z * 96) // 24
    source = by_y * 192 + by_z * 24 + (column - by_z * 96 - by_y * 24)
    order = lax.broadcasted_iota(jnp.int32, (D, D), 0) == source
    order = order.astype(F32).astype(BF16)
    for k in range(8):
        rot_send[k] = rot_buf[:, k * 96 : (k + 1) * 96]
    qv.advance(1)
    o_x.along_y.begin()
    ey.begin()
    u_z.advance(1)
    iy.done()

    n_slots = 8
    wanted = jnp.concatenate([ids_out[i, tens] for i in range(N_Y)], axis=0)
    owners = jnp.floor(wanted * (1.0 / 1024))
    lists = wanted - owners * 1024.0
    own = (owners == dp.astype(F32)).astype(F32)
    one = lax.broadcasted_iota(jnp.int32, (64, 64), 0)
    two = lax.broadcasted_iota(jnp.int32, (64, 64), 1)
    earlier = ((one > two) & (one // 16 == two // 16)).astype(BF16)
    rank = jnp.dot(earlier, own.astype(BF16), preferred_element_type=F32)
    hots = []
    for r in range(2):
        named = jnp.where((own > 0.5) & (rank == float(r)), lists + 1.0, 0.0)
        named = jnp.sum(named.reshape(N_Y, 16, 128), axis=1) - 1.0
        hots.append(named)
    named = jnp.concatenate(hots, axis=0)
    places = lax.broadcasted_iota(jnp.int32, (n_slots, 1024), 1).astype(F32)
    hot = places == named[:, 0:1]
    mine_rows[:, 0:D] = pick(hot.astype(F32).astype(BF16), old_buf[...])
    mine_rows[:, D : D + 128] = jnp.broadcast_to(
        jnp.sum(
            jnp.where(hot, weight_ref[...].astype(F32).reshape(1, 1024), 0.0),
            axis=1,
            keepdims=True,
        ),
        (n_slots, 128),
    )
    qv.advance(2)
    k_x.done_x()
    dx.done()
    d_y.begin()
    o_x.begin_x()
    ey.done()
    ex.begin()
    qv.done()
    k_x.done()

    turn_numbers = [sems.take() for _ in range(N_Y)]
    turn_to = [((lax.rem(y + k, N_Y)) * N_Z + tens, z) for k in range(N_Y)]
    rot_numbers = [sems.take() for _ in range(7)]
    row_numbers = [sems.take() for _ in range(7)]
    rot_place = pl.ds(pl.multiple_of(tens * 96, 32), 96)

    def send_rows_and_rotation():
        for k in range(1, N_Y):
            sems.send(mine_rows, turn_numbers[k], turn_to[k], dst=owner_rows.at[y])

        @pl.when(jnp.logical_not(is_turn_self))
        def _():
            copy = sems._copy(mine_rows, owner_rows.at[y], turn_numbers[0], turn_to[0])
            copy.start()
            copy.wait_send()

        @pl.when(is_turn_self)
        def _():
            owner_rows[y] = mine_rows[...]

        rot_out[rot_place, :] = rot_send[tens]
        for k in range(1, 8):
            other = lax.rem(tens + k, 8)
            sems.send(
                rot_send.at[other], rot_numbers[k - 1], peers[k - 1], dst=rot_out.at[rot_place]
            )

    def share_rows():
        @pl.when(jnp.logical_not(is_turn_self))
        def _():
            sems.arrived(owner_rows.at[y], turn_numbers[0], turn_to[0])

        for k in range(1, N_Y):
            sems.arrived(
                owner_rows.at[lax.rem(y + N_Y - k, N_Y)], turn_numbers[k], turn_to[k]
            )
        for r in range(2):
            for i in range(N_Y):
                rows_out[tens, r * N_Y + i : r * N_Y + i + 1, :] = owner_rows[
                    i, pl.ds(r * N_Y + y, 1), :
                ]
        for k in range(1, 8):
            sems.send(rows_out.at[tens], row_numbers[k - 1], peers[k - 1])

    def share_e():
        ex.done()
        sems.send(w_e.at[pl.ds(core * 4, 4)], e_hand, sibling)

    def project(c):
        for at in range(2):
            part = jnp.dot(x_ref[...], w_a[c * 2 + at], preferred_element_type=F32).astype(BF16)
            if at == 0:
                part = part * 0.125
            qkv[c * 3 + at] = part
        for j in range(3):
            part = jnp.dot(x_ref[...], w_k[c, j], preferred_element_type=F32).astype(BF16)
            qkv[c * 3 + 2, :, j * 128 : (j + 1) * 128] = part

    lane = lax.broadcasted_iota(jnp.int32, (1, 128), 1)
    low = (lane < 64).astype(F32).astype(BF16)
    both_halves = (low, 1 - low)
    key_at = lax.broadcasted_iota(jnp.int32, (1, L), 1)

    def attend(p, c, j):
        keys_ok = key_at < lens_ref[2 * tens + p]
        tokens = slice(p * L, (p + 1) * L)
        columns = slice(j * 128, (j + 1) * 128)
        q = qkv[c * 3, tokens, columns]
        v = qkv[c * 3 + 1, tokens, columns]
        k = qkv[c * 3 + 2, tokens, columns]
        total = None
        for half in both_halves:
            scores = lax.dot_general(
                q * half, k, (((1,), (1,)), ((), ())), preferred_element_type=F32
            )
            scores = jnp.where(keys_ok, scores, -1e30)
            powers = jnp.exp(scores - jnp.max(scores, axis=1, keepdims=True))
            scale = 1.0 / jnp.sum(powers, axis=1, keepdims=True)
            probs = (powers * scale).astype(BF16)
            part = jnp.dot(probs, v * half, preferred_element_type=F32)
            total = part if total is None else total + part
        ctx[tokens, c * SLAB + j * 128 : c * SLAB + (j + 1) * 128] = total.astype(BF16)

    def mix(b):
        tokens = slice(b * L, (b + 1) * L)
        mixed = jnp.concatenate(
            [
                jnp.dot(ctx[tokens, :], w_o[c, j], preferred_element_type=F32)
                for c in range(2)
                for j in range(3)
            ],
            axis=1,
        )
        values = x_ref[tokens, :].astype(F32) + mixed
        centered = values - jnp.mean(values, axis=1, keepdims=True)
        spread = jnp.mean(centered * centered, axis=1, keepdims=True)
        normed = centered * lax.rsqrt(spread + EPS) * gain_one_ref[...].reshape(
            1, D
        ) + shift_one_ref[...].reshape(1, D)
        normed = normed.astype(BF16)
        acc[tokens, :] = normed.astype(F32)
        first[tokens, :] = jnp.dot(normed, order, preferred_element_type=F32).astype(BF16)

    u_z.advance(2)
    project(0)
    send_rows_and_rotation()
    project(1)
    steps = {
        1: lambda: u_z.advance(3),
        3: o_x.done_x,
        5: share_e,
        6: share_rows,
        8: lambda: u_z.advance(4),
        11: lambda: d_y.advance(1),
    }
    for n, (c, p, j) in enumerate(
        (c, p, j) for c in range(2) for p in range(2) for j in range(3)
    ):
        attend(p, c, j)
        if n in steps:
            steps[n]()
    o_x.done()
    mix(0)
    mix(1)
    u_z.done()

    def raise_slabs(n, carry):
        for s in (2 * n, 2 * n + 1):
            for b in range(2):
                tokens = slice(b * L, (b + 1) * L)
                up = jnp.dot(first[tokens, :], w_u[s], preferred_element_type=F32)
                half = 0.5 * up
                act[s, tokens, :] = (half + half * lax.erf(up * (0.5**0.5))).astype(BF16)
        return carry

    def lower_slabs(n, carry):
        total = acc[...]
        for s in (2 * n, 2 * n + 1):
            total = total + lax.dot_general(
                act[s, :, 0:256], w_d[s], (((1,), (1,)), ((), ())), preferred_element_type=F32
            )
        last = jnp.concatenate([act[s, :, 256:SLAB] for s in (2 * n, 2 * n + 1)], axis=1)
        weights = jnp.concatenate([w_e[s] for s in (2 * n, 2 * n + 1)], axis=1)
        acc[...] = total + lax.dot_general(
            last, weights, (((1,), (1,)), ((), ())), preferred_element_type=F32
        )
        return carry

    lax.fori_loop(0, 4, raise_slabs, 0)
    d_y.advance(2)
    sems.arrived(w_e.at[pl.ds((1 - core) * 4, 4)], e_hand, sibling)
    d_y.done()
    lax.fori_loop(0, 4, lower_slabs, 0)

    token_at = lax.broadcasted_iota(jnp.int32, (L, 1), 0)
    for p in range(2):
        length = lens_ref[2 * tens + p]
        values = acc[p * L : (p + 1) * L, :]
        centered = values - jnp.mean(values, axis=1, keepdims=True)
        spread = jnp.mean(centered * centered, axis=1, keepdims=True)
        scaled = centered * lax.rsqrt(spread + EPS)
        pooled = jnp.sum(jnp.where(token_at < length, scaled, 0.0), axis=0, keepdims=True)
        emb = pooled / length.astype(F32) * gain_two_ref[...].reshape(1, D)
        emb_group[tens, p : p + 1, :] = emb + shift_two_ref[...].reshape(1, D)

    group_numbers = [sems.take() for _ in range(7)]
    for k in range(1, 8):
        sems.send(emb_group.at[tens], group_numbers[k - 1], peers[k - 1])
    sems.finish()
    for k in range(1, 8):
        origin = lax.rem(tens + 8 - k, 8)
        place = pl.ds(pl.multiple_of(origin * 96, 32), 96)
        sems.arrived(rot_out.at[place], rot_numbers[k - 1], peers[k - 1])
        sems.arrived(rows_out.at[origin], row_numbers[k - 1], peers[k - 1])
    for k in range(1, 8):
        other = lax.rem(tens + 8 - k, 8)
        sems.arrived(emb_group.at[other], group_numbers[k - 1], peers[k - 1])
    for t in range(8):
        both = emb_group[t]
        @pl.when(core == 0)
        def _():
            emb_out[0, y, z, 2 * t : 2 * t + 2, :] = both[:, :SLAB]
        @pl.when(core == 1)
        def _():
            emb_out[1, y, z, 2 * t : 2 * t + 2, :] = both[:, SLAB:]
    ze = Direct(sems, N_Z, z, at_z, lambda i: emb_out.at[core, y, i])

    def emb_parts(c, i):
        return emb_out.at[c, i, pl.ds(0, 4)], emb_out.at[c, i, pl.ds(4, 4)]

    ye = Spread(
        sems, N_Y, y, y_right, y_left, sibling,
        lambda i: emb_parts(core, i), lambda i: emb_parts(1 - core, i),
    )
    ze.begin()
    ze.done()
    ye.begin()
    ye.advance(1)
    ye.advance(2)
    ye.done()
    sems.finish()


def finish_kernel(emb_ref, ids_ref, rows_ref, rot_ref, weight_ref, old_ref, rotated_ref, centroids_ref, slot_ids, slots):
    step = pl.program_id(0)
    dp = lax.axis_index("dp")

    @pl.when(step == 0)
    def _():
        ids_row = jnp.transpose(ids_ref[...])[0:8, :]
        ids = ids_ref[pl.ds(pl.multiple_of(dp * 16, 16), 16), :]
        owners = jnp.floor(ids * (1.0 / 1024))
        owner_y = jnp.floor(owners * (1.0 / N_Z))
        owner_z = owners - owner_y * N_Z
        one = lax.broadcasted_iota(jnp.int32, (16, 16), 0)
        two = lax.broadcasted_iota(jnp.int32, (16, 16), 1)
        owners_row = jnp.sum(jnp.where(one == two, owners[:, 0:16], 0.0), axis=0, keepdims=True)
        rank = jnp.sum(
            ((owners[:, 0:16] == owners_row) & (two < one)).astype(F32), axis=1, keepdims=True
        )
        place = owner_z * 8.0 + rank * N_Y + owner_y
        spots = lax.broadcasted_iota(jnp.int32, (16, 64), 1).astype(F32)
        hot = (place[:, 0:64] == spots).astype(F32).astype(BF16)
        old = pick(hot, rows_ref[...])
        same = ids[:, 0:1] == ids_row[0:1, :]
        counts = jnp.sum(same.astype(F32), axis=1, keepdims=True)
        mine = jnp.floor(ids_row * (1.0 / 1024)) == dp.astype(F32)
        before = lax.broadcasted_iota(jnp.int32, (ROWS, ROWS), 0) < lax.broadcasted_iota(
            jnp.int32, (ROWS, ROWS), 1
        )
        spot = jnp.dot(
            mine.astype(F32).astype(BF16),
            before.astype(F32).astype(BF16),
            preferred_element_type=F32,
        )
        numbers = lax.broadcasted_iota(jnp.int32, (64, ROWS), 0).astype(F32)
        placed = (numbers == spot[0:1, :]) & mine[0:1, :]
        named = jnp.sum(jnp.where(placed, ids_row[0:1, :] + 1.0, 0.0), axis=1, keepdims=True)
        named = jnp.concatenate([named - 1.0, jnp.full((64, 1), -1.0, F32)], axis=0)
        slot_ids[...] = jnp.transpose(jnp.broadcast_to(named, (128, 128)))[0:8, :]
        taken = jnp.concatenate([same.astype(F32), placed.astype(F32)], axis=0).astype(BF16)
        weight = old[:, D : D + 1]
        result = None
        for h in range(2):
            picked = pick(taken, emb_ref[h])
            sums = picked[0:16, :]
            for k, part in enumerate(split3(picked[16:80, :])):
                slots[k * 64 : (k + 1) * 64, h * SLAB : (h + 1) * SLAB] = part
            centroids = (weight * old[:, h * SLAB : (h + 1) * SLAB] + sums) / (weight + counts)
            resid = emb_ref[h, pl.ds(pl.multiple_of(dp * 16, 16), 16), :] - centroids
            part = jnp.dot(
                resid,
                rot_ref[h * SLAB : (h + 1) * SLAB, :],
                precision=lax.Precision.HIGHEST,
                preferred_element_type=F32,
            )
            result = part if result is None else result + part
        rotated_ref[...] = result

    one = lax.broadcasted_iota(jnp.int32, (128, 128), 0)
    two = lax.broadcasted_iota(jnp.int32, (128, 128), 1)
    weight = jnp.concatenate(
        [
            jnp.sum(
                jnp.where(one == two, weight_ref[pl.ds(step * 4 + i, 1), :].astype(F32), 0.0),
                axis=1,
                keepdims=True,
            )
            for i in range(4)
        ],
        axis=0,
    )
    number = lax.broadcasted_iota(jnp.int32, (512, 64), 0) + dp * 1024 + step * 512
    hot = (number.astype(F32) == slot_ids[0:1, 0:64]).astype(F32)
    counts = jnp.sum(hot, axis=1, keepdims=True)
    hot = jnp.concatenate([hot, hot, hot], axis=1).astype(BF16)
    for h in range(2):
        columns = slice(h * SLAB, (h + 1) * SLAB)
        sums = jnp.dot(hot, slots[:, columns], preferred_element_type=F32)
        centroids_ref[:, columns] = (weight * old_ref[:, columns] + sums) / (weight + counts)


VMEM = pl.BlockSpec(memory_space=pltpu.VMEM)
HBM = pl.BlockSpec(memory_space=pltpu.HBM)


def local(
    hidden,
    lengths,
    owner_of,
    list_local,
    old_weight,
    old_centroids,
    w_qkv,
    w_out,
    gain_one,
    shift_one,
    w_up,
    w_down,
    gain_two,
    shift_two,
    rotation,
):
    vmem = pltpu.VMEM
    emb, ids, rows, rot = pl.pallas_call(
        encode_kernel,
        out_shape=(
            jax.ShapeDtypeStruct((2, N_Y, N_Z, 16, SLAB), F32),
            jax.ShapeDtypeStruct((N_Y, N_Z, 16, 128), F32),
            jax.ShapeDtypeStruct((8, 8, D + 128), F32),
            jax.ShapeDtypeStruct((D, 96), F32),
        ),
        in_specs=[HBM] * 15,
        out_specs=(VMEM,) * 4,
        scratch_shapes=[
            vmem((4, D, SLAB), BF16),
            vmem((8, D, SLAB), BF16),
            vmem((8, D, 256), BF16),
            vmem((8, D, 128), BF16),
            vmem((2, 3, D, 128), BF16),
            vmem((2, 3, D, 128), BF16),
            vmem((N_Z, 24, 2 * SLAB + 128), BF16),
            vmem((N_Y, 4, 24, SLAB), BF16),
            vmem((N_Z, 24, SLAB + 128), BF16),
            vmem((192, SLAB), F32),
            pltpu.SMEM((16,), jnp.int32),
            pltpu.SMEM((16,), jnp.int32),
            pltpu.SMEM((16,), jnp.int32),
            vmem((1024,), jnp.int32),
            vmem((D,), F32),
            vmem((D,), F32),
            vmem((D,), F32),
            vmem((D,), F32),
            vmem((ROWS, D), BF16),
            vmem((96, D), F32),
            vmem((1024, D), F32),
            vmem((8, 96, 96), F32),
            vmem((8, D + 128), F32),
            vmem((N_Y, 8, D + 128), F32),
            vmem((8, 2, D), F32),
            vmem((6, ROWS, SLAB), BF16),
            vmem((ROWS, D), BF16),
            vmem((ROWS, D), BF16),
            vmem((8, ROWS, SLAB), BF16),
            vmem((ROWS, D), F32),
            pltpu.SemaphoreType.DMA((N_COPIES,)),
            pltpu.SemaphoreType.DMA((N_COPIES,)),
            pltpu.SemaphoreType.DMA((17,)),
        ],
        compiler_params=pltpu.CompilerParams(
            collective_id=0, has_side_effects=True, vmem_limit_bytes=60 * 2**20
        ),
    )(
        lengths,
        owner_of.reshape(16),
        list_local,
        old_weight,
        gain_one,
        shift_one,
        gain_two,
        shift_two,
        hidden.reshape(ROWS, D),
        old_centroids,
        w_qkv,
        w_out,
        w_up,
        w_down.T,
        rotation,
    )
    whole = lambda *shape: pl.BlockSpec(shape, lambda i: (0,) * len(shape))
    return pl.pallas_call(
        finish_kernel,
        grid=(2,),
        out_shape=(
            jax.ShapeDtypeStruct((16, 96), F32),
            jax.ShapeDtypeStruct((1024, D), F32),
        ),
        in_specs=[
            whole(2, ROWS, SLAB),
            whole(ROWS, 128),
            whole(64, D + 128),
            whole(D, 96),
            whole(8, 128),
            pl.BlockSpec((512, D), lambda i: (i, 0)),
        ],
        out_specs=(whole(16, 96), pl.BlockSpec((512, D), lambda i: (i, 0))),
        scratch_shapes=[vmem((8, 128), F32), vmem((192, D), BF16)],
        compiler_params=pltpu.CompilerParams(vmem_limit_bytes=60 * 2**20),
    )(
        emb.reshape(2, ROWS, SLAB),
        ids.reshape(ROWS, 128),
        rows.reshape(64, D + 128),
        rot,
        old_weight.reshape(8, 128),
        old_centroids,
    )


def solution(mesh):
    return jax.shard_map(
        local,
        mesh=mesh,
        in_specs=(
            P(("dp", "tensor"), None, None),
            P("dp"),
            P("dp", None),
            P("dp"),
            P("dp"),
            P("dp", None),
            P("dp", None),
            P("dp", None),
            P(),
            P(),
            P("dp", "tensor"),
            P("tensor", "dp"),
            P(),
            P(),
            P("tensor", None),
        ),
        out_specs=(P("dp", "tensor"), P("dp", None)),
        check_vma=False,
    )
```

```python
import functools

import jax
import jax.numpy as jnp
from jax import lax
from jax.experimental import pallas as pl
from jax.experimental.pallas import tpu as pltpu
from jax.sharding import PartitionSpec as P

EPS = 1e-05
MESH = pl.DeviceIdType.MESH
F32 = jnp.float32
BF16 = jnp.bfloat16

L = 256
D = 768
SLAB = 384
N_Y = 4
N_Z = 8
N_X = 4
ROWS = 512


def split3(values):
    high = values.astype(BF16)
    rest = values - high.astype(F32)
    mid = rest.astype(BF16)
    low = (rest - mid.astype(F32)).astype(BF16)
    return high, mid, low


def pick(hot, values):
    parts = split3(values)
    return sum(jnp.dot(hot, part, preferred_element_type=F32) for part in parts)


class Ring:
    def __init__(self, sems, n, me, right, left, parts):
        self.n, self.me, self.right, self.left = n, me, right, left
        self.parts = parts
        self.sems = sems
        self.ids = [[(sems.take(), sems.take()) for _ in range(2)] for _ in range(n // 2)]

    def _at(self, offset):
        return lax.rem(self.me + offset + self.n, self.n)

    def start(self, step, part):
        a, b = self.ids[step - 1][part]
        last = step == self.n // 2
        if not last or part == 0:
            self.sems.send(self.parts(self._at(1 - step))[part], a, self.right)
        if not last or part == 1:
            self.sems.send(self.parts(self._at(step - 1))[part], b, self.left)

    def wait(self, step, part):
        a, b = self.ids[step - 1][part]
        last = step == self.n // 2
        if not last or part == 0:
            self.sems.arrived(self.parts(self._at(-step))[part], a, self.right)
        if not last or part == 1:
            self.sems.arrived(self.parts(self._at(step))[part], b, self.left)

    def begin(self):
        for part in range(2):
            self.start(1, part)

    def advance(self, step):
        for part in range(2):
            self.wait(step, part)
            if step < self.n // 2:
                self.start(step + 1, part)


class Direct:
    def __init__(self, sems, n, me, device, block):
        self.sems, self.n, self.me, self.device, self.block = sems, n, me, device, block
        self.numbers = [sems.take() for _ in range(n)]

    def begin(self):
        offsets = sorted(range(1, self.n), key=lambda k: -min(k, self.n - k))
        for k in offsets:
            i = lax.rem(self.me + k, self.n)
            self.sems.send(self.block(self.me), self.numbers[k], self.device(i))

    def done(self):
        for k in range(1, self.n):
            i = lax.rem(self.me + self.n - k, self.n)
            self.sems.arrived(self.block(i), self.numbers[k], self.device(i))


class Copies:
    def __init__(self, send, recv):
        self.send_sems, self.recv_sems = send, recv
        self.count = 0
        self.started = []

    def take(self):
        self.count += 1
        return self.count - 1

    def _copy(self, src, dst, number, device):
        return pltpu.make_async_remote_copy(
            src_ref=src,
            dst_ref=dst,
            send_sem=self.send_sems.at[number],
            recv_sem=self.recv_sems.at[number],
            device_id=device,
            device_id_type=MESH,
        )

    def send(self, src, number, device, dst=None):
        copy = self._copy(src, src if dst is None else dst, number, device)
        copy.start()
        self.started.append((None, copy.wait_send))

    def send_if(self, condition, src, number, device):
        @pl.when(condition)
        def _():
            self._copy(src, src, number, device).start()

        self.started.append(
            (condition, lambda: self._copy(src, src, number, device).wait_send())
        )

    def arrived(self, ref, number, device):
        self._copy(ref, ref, number, device).wait_recv()

    def finish(self):
        for condition, wait in self.started:
            if condition is None:
                wait()
            else:
                pl.when(condition)(wait)
        self.started = []


N_COPIES = 288


class Spread(Ring):
    def __init__(self, sems, n, me, right, left, sibling, mine, theirs):
        super().__init__(sems, n, me, right, left, mine)
        self.sibling, self.theirs = sibling, theirs
        self.hands = [(sems.take(), sems.take()) for _ in range(n)]

    def _hand(self, offset, part):
        number = self.hands[offset % self.n][part]
        self.sems.send(self.parts(self._at(offset))[part], number, self.sibling)

    def begin_part(self, part):
        self.start(1, part)
        self._hand(0, part)

    def begin(self):
        for part in range(2):
            self.begin_part(part)

    def advance(self, step):
        for part in range(2):
            self.wait(step, part)
            if step < self.n // 2:
                self.start(step + 1, part)
                self._hand(-step, part)
            self._hand(step, part)

    def done(self, offsets=None):
        for offset in range(self.n) if offsets is None else offsets:
            for part in range(2):
                i = self._at(offset)
                self.sems.arrived(self.theirs(i)[part], self.hands[offset][part], self.sibling)


class Third:
    def __init__(self, sems, buf, x, y, core, at_x, at_y, y_rows, sibling):
        self.sems, self.buf, self.core, self.at_x, self.sibling = sems, buf, core, at_x, sibling
        self.x, self.tile = x, jnp.minimum(x, 2)
        self.along_y = Direct(
            sems, N_Y, y, at_y, lambda i: buf.at[core, self.tile, y_rows(i)]
        )
        self.numbers = [sems.take() for _ in range(N_X)]
        self.hands = [sems.take() for _ in range(N_X)]
        self.origins = [lax.rem(x + N_X - k, N_X) for k in range(N_X)]
        self.comes = [
            (i < 3) & jnp.logical_not((x == 3) & (i == 2)) for i in self.origins
        ]

    def begin_x(self):
        self.along_y.done()
        mine = self.buf.at[self.core, self.tile]
        for k in range(1, N_X):
            goes = self.x < 3
            if k == 1:
                goes = self.x < 2
            self.sems.send_if(goes, mine, self.numbers[k], self.at_x(lax.rem(self.x + k, N_X)))
        self.sems.send(mine, self.hands[0], self.sibling)

    def done_x(self):
        for k in range(1, N_X):
            ref = self.buf.at[self.core, jnp.minimum(self.origins[k], 2)]

            @pl.when(self.comes[k])
            def _():
                self.sems.arrived(ref, self.numbers[k], self.at_x(self.origins[k]))

            self.sems.send_if(self.comes[k], ref, self.hands[k], self.sibling)

    def done(self):
        self.sems.arrived(self.buf.at[1 - self.core, self.tile], self.hands[0], self.sibling)
        for k in range(1, N_X):
            ref = self.buf.at[1 - self.core, jnp.minimum(self.origins[k], 2)]

            @pl.when(self.comes[k])
            def _():
                self.sems.arrived(ref, self.hands[k], self.sibling)


def encode_kernel(
    lens_any,
    owner_any,
    list_any,
    weight_any,
    gain_one_any,
    shift_one_any,
    gain_two_any,
    shift_two_any,
    x_any,
    old_ref,
    wqkv_ref,
    wout_ref,
    wup_ref,
    wdown_ref,
    rot_ref,
    emb_out,
    ids_out,
    rows_out,
    rot_out,
    w_a,
    w_u,
    w_d,
    w_e,
    w_k,
    w_o,
    z_a,
    y_u,
    z_d,
    turned,
    lens_ref,
    owner_ref,
    list_ref,
    weight_ref,
    gain_one_ref,
    shift_one_ref,
    gain_two_ref,
    shift_two_ref,
    x_ref,
    rot_buf,
    old_buf,
    rot_send,
    mine_rows,
    owner_rows,
    emb_group,
    qkv,
    ctx,
    first,
    act,
    acc,
    send_sems,
    recv_sems,
    local_sems,
):
    dp = lax.axis_index("dp")
    tens = lax.axis_index("tensor")
    y, z = dp // N_Z, lax.rem(dp, N_Z)
    x, core = tens // 2, lax.rem(tens, 2)

    def at_y(i):
        return (i * N_Z + z, tens)

    def at_z(i):
        return (y * N_Z + i, tens)

    def at_x(i):
        return (dp, 2 * i + core)

    y_right, y_left = at_y(lax.rem(y + 1, N_Y)), at_y(lax.rem(y + N_Y - 1, N_Y))
    z_right, z_left = at_z(lax.rem(z + 1, N_Z)), at_z(lax.rem(z + N_Z - 1, N_Z))
    peers = [(dp, lax.rem(tens + k, 8)) for k in range(1, 8)]
    sibling = (dp, 2 * x + 1 - core)
    is_turn_self = tens == z
    turn = [(i * N_Z + tens, z) for i in range(N_Y)]

    third = jnp.minimum(x, 2)

    def cut(ref, at, tile=None):
        if tile is None:
            return ref.at[:, pl.ds(pl.multiple_of(at * SLAB, 128), SLAB)]
        return ref.at[:, pl.ds(pl.multiple_of(at * SLAB + tile * 128, 128), 128)]

    loads = [
        (cut(wqkv_ref, core), z_a.at[z, :, pl.ds(0, SLAB)]),
        (cut(wqkv_ref, 4 + core), z_a.at[z, :, pl.ds(SLAB, SLAB)]),
        (cut(wqkv_ref, 2 + core, third), z_a.at[z, :, pl.ds(2 * SLAB, 128)]),
        (wup_ref, y_u.at[y, x]),
        (wdown_ref, z_d.at[z, :, pl.ds(0, SLAB)]),
        (cut(wout_ref, core, third), z_d.at[z, :, pl.ds(SLAB, 128)]),
        (owner_any, owner_ref),
        (list_any, list_ref),
        (lens_any, lens_ref),
        (x_any, x_ref),
        (gain_one_any, gain_one_ref),
        (shift_one_any, shift_one_ref),
        (gain_two_any, gain_two_ref),
        (shift_two_any, shift_two_ref),
        (weight_any, weight_ref),
        (rot_ref, rot_buf),
        (old_ref, old_buf),
    ]
    loads = [
        pltpu.make_async_copy(src, dst, local_sems.at[i]) for i, (src, dst) in enumerate(loads)
    ]
    for load in loads:
        load.start()

    barrier = pltpu.get_barrier_semaphore()
    others = [at_y(lax.rem(y + k, N_Y)) for k in range(1, N_Y)]
    others += [at_z(lax.rem(z + k, N_Z)) for k in range(1, N_Z)]
    for device in others + peers:
        pl.semaphore_signal(barrier, inc=1, device_id=device, device_id_type=MESH)
    for i in range(N_Y):
        @pl.when(jnp.logical_not(jnp.logical_and(is_turn_self, y == i)))
        def _():
            pl.semaphore_signal(barrier, inc=1, device_id=turn[i], device_id_type=MESH)

    for load in loads[:6]:
        load.wait()
    pl.semaphore_wait(barrier, 17 + N_Y - is_turn_self.astype(jnp.int32))

    sems = Copies(send_sems, recv_sems)

    def z_rows(i):
        return pl.ds(pl.multiple_of(i * 96, 32), 96)

    def y_rows(i):
        return pl.ds(pl.multiple_of(i * 192, 64), 192)

    def y_last(buf, count):
        half = count // 2

        def parts(c, i):
            return [buf.at[pl.ds(c * count + k, half), y_rows(i)] for k in (0, half)]

        return Spread(
            sems, N_Y, y, y_right, y_left, sibling,
            lambda i: parts(core, i), lambda i: parts(1 - core, i),
        )

    def z_last(buf, count):
        half = count // 2

        def parts(c, i):
            return [buf.at[pl.ds(c * count + k, half), z_rows(i)] for k in (0, half)]

        return Spread(
            sems, N_Z, z, z_right, z_left, sibling,
            lambda i: parts(core, i), lambda i: parts(1 - core, i),
        )

    def assemble(blocks, full):
        wide = full.shape[-1]
        for i, block in enumerate(blocks):
            turned[i * 24 : (i + 1) * 24, 0:wide] = block.astype(F32)
        full[...] = turned[0 : 24 * len(blocks), 0:wide].astype(BF16)

    az = Direct(sems, N_Z, z, at_z, lambda i: z_a.at[i])
    dz = Direct(sems, N_Z, z, at_z, lambda i: z_d.at[i])
    ux = Direct(sems, N_X, x, at_x, lambda i: y_u.at[y, i])
    uy = Direct(sems, N_Y, y, at_y, lambda i: y_u.at[i])
    dx = Direct(sems, N_X, x, at_x, lambda i: w_d.at[core * 4 + i, y_rows(y)])
    ey = Direct(sems, N_Y, y, at_y, lambda i: w_e.at[core * 4 + x, y_rows(i)])
    ex = Direct(sems, N_X, x, at_x, lambda i: w_e.at[core * 4 + i])
    e_hand = sems.take()
    iz = Direct(sems, N_Z, z, at_z, lambda i: ids_out.at[y, i])
    iy = Direct(sems, N_Y, y, at_y, lambda i: ids_out.at[i])
    qv, u_z, d_y = y_last(w_a, 2), z_last(w_u, 4), y_last(w_d, 4)
    k_x = Third(sems, w_k, x, y, core, at_x, at_y, y_rows, sibling)
    o_x = Third(sems, w_o, x, y, core, at_x, at_y, y_rows, sibling)

    az.begin()
    ux.begin()
    dz.begin()
    for load in loads[6:8]:
        load.wait()
    ids_rows = [
        jnp.full((1, 128), owner_ref[i] * 1024 + list_ref[i], jnp.int32) for i in range(16)
    ]
    ids_out[y, z] = jnp.concatenate(ids_rows, axis=0).astype(F32)
    iz.begin()
    ux.done()
    uy.begin()
    az.done()
    assemble(
        [z_a[i, :, 2 * SLAB : 2 * SLAB + 128] for i in range(N_Z)],
        w_k.at[core, third, y_rows(y)],
    )
    k_x.along_y.begin()
    for s in range(2):
        assemble(
            [z_a[i, :, s * SLAB : (s + 1) * SLAB] for i in range(N_Z)],
            w_a.at[core * 2 + s, y_rows(y)],
        )
        qv.begin_part(s)
    uy.done()
    for s in range(4):
        assemble([y_u[i, s] for i in range(N_Y)], w_u.at[core * 4 + s, z_rows(z)])
    u_z.begin()
    k_x.begin_x()
    dz.done()
    assemble([z_d[i, :, 0:256] for i in range(N_Z)], w_d.at[core * 4 + x, y_rows(y)])
    dx.begin()
    assemble([z_d[i, :, 256:SLAB] for i in range(N_Z)], w_e.at[core * 4 + x, y_rows(y)])
    assemble(
        [z_d[i, :, SLAB : SLAB + 128] for i in range(N_Z)], w_o.at[core, third, y_rows(y)]
    )
    o_x.along_y.begin()
    ey.begin()
    iz.done()
    iy.begin()

    for load in loads[8:]:
        load.wait()
    column = lax.broadcasted_iota(jnp.int32, (1, D), 1)
    by_z = column // 96
    by_y = (column - by_z * 96) // 24
    source = by_y * 192 + by_z * 24 + (column - by_z * 96 - by_y * 24)
    order = lax.broadcasted_iota(jnp.int32, (D, D), 0) == source
    order = order.astype(F32).astype(BF16)
    for k in range(8):
        rot_send[k] = rot_buf[:, k * 96 : (k + 1) * 96]
    qv.advance(1)
    o_x.begin_x()
    u_z.advance(1)
    iy.done()

    n_slots = 8
    wanted = jnp.concatenate([ids_out[i, tens] for i in range(N_Y)], axis=0)
    owners = jnp.floor(wanted * (1.0 / 1024))
    lists = wanted - owners * 1024.0
    own = (owners == dp.astype(F32)).astype(F32)
    one = lax.broadcasted_iota(jnp.int32, (64, 64), 0)
    two = lax.broadcasted_iota(jnp.int32, (64, 64), 1)
    earlier = ((one > two) & (one // 16 == two // 16)).astype(BF16)
    rank = jnp.dot(earlier, own.astype(BF16), preferred_element_type=F32)
    hots = []
    for r in range(2):
        named = jnp.where((own > 0.5) & (rank == float(r)), lists + 1.0, 0.0)
        named = jnp.sum(named.reshape(N_Y, 16, 128), axis=1) - 1.0
        hots.append(named)
    named = jnp.concatenate(hots, axis=0)
    places = lax.broadcasted_iota(jnp.int32, (n_slots, 1024), 1).astype(F32)
    hot = places == named[:, 0:1]
    mine_rows[:, 0:D] = pick(hot.astype(F32).astype(BF16), old_buf[...])
    mine_rows[:, D : D + 128] = jnp.broadcast_to(
        jnp.sum(
            jnp.where(hot, weight_ref[...].astype(F32).reshape(1, 1024), 0.0),
            axis=1,
            keepdims=True,
        ),
        (n_slots, 128),
    )
    qv.advance(2)
    k_x.done_x()
    dx.done()
    d_y.begin()
    ey.done()
    ex.begin()
    qv.done()
    k_x.done()

    turn_numbers = [sems.take() for _ in range(N_Y)]
    turn_to = [((lax.rem(y + k, N_Y)) * N_Z + tens, z) for k in range(N_Y)]
    rot_numbers = [sems.take() for _ in range(7)]
    row_numbers = [sems.take() for _ in range(7)]
    rot_place = pl.ds(pl.multiple_of(tens * 96, 32), 96)

    def send_rows_and_rotation():
        for k in range(1, N_Y):
            sems.send(mine_rows, turn_numbers[k], turn_to[k], dst=owner_rows.at[y])

        @pl.when(jnp.logical_not(is_turn_self))
        def _():
            copy = sems._copy(mine_rows, owner_rows.at[y], turn_numbers[0], turn_to[0])
            copy.start()
            copy.wait_send()

        @pl.when(is_turn_self)
        def _():
            owner_rows[y] = mine_rows[...]

        rot_out[rot_place, :] = rot_send[tens]
        for k in range(1, 8):
            other = lax.rem(tens + k, 8)
            sems.send(
                rot_send.at[other], rot_numbers[k - 1], peers[k - 1], dst=rot_out.at[rot_place]
            )

    def share_rows():
        @pl.when(jnp.logical_not(is_turn_self))
        def _():
            sems.arrived(owner_rows.at[y], turn_numbers[0], turn_to[0])

        for k in range(1, N_Y):
            sems.arrived(
                owner_rows.at[lax.rem(y + N_Y - k, N_Y)], turn_numbers[k], turn_to[k]
            )
        for r in range(2):
            for i in range(N_Y):
                rows_out[tens, r * N_Y + i : r * N_Y + i + 1, :] = owner_rows[
                    i, pl.ds(r * N_Y + y, 1), :
                ]
        for k in range(1, 8):
            sems.send(rows_out.at[tens], row_numbers[k - 1], peers[k - 1])

    def share_e():
        ex.done()
        sems.send(w_e.at[pl.ds(core * 4, 4)], e_hand, sibling)

    def project(c):
        for at in range(2):
            part = jnp.dot(x_ref[...], w_a[c * 2 + at], preferred_element_type=F32).astype(BF16)
            if at == 0:
                part = part * 0.125
            qkv[c * 3 + at] = part
        for j in range(3):
            part = jnp.dot(x_ref[...], w_k[c, j], preferred_element_type=F32).astype(BF16)
            qkv[c * 3 + 2, :, j * 128 : (j + 1) * 128] = part

    lane = lax.broadcasted_iota(jnp.int32, (1, 128), 1)
    low = (lane < 64).astype(F32).astype(BF16)
    both_halves = (low, 1 - low)
    key_at = lax.broadcasted_iota(jnp.int32, (1, L), 1)

    def attend(p, c, j):
        keys_ok = key_at < lens_ref[2 * tens + p]
        tokens = slice(p * L, (p + 1) * L)
        columns = slice(j * 128, (j + 1) * 128)
        q = qkv[c * 3, tokens, columns]
        v = qkv[c * 3 + 1, tokens, columns]
        k = qkv[c * 3 + 2, tokens, columns]
        total = None
        for half in both_halves:
            scores = lax.dot_general(
                q * half, k, (((1,), (1,)), ((), ())), preferred_element_type=F32
            )
            scores = jnp.where(keys_ok, scores, -1e30)
            powers = jnp.exp(scores - jnp.max(scores, axis=1, keepdims=True))
            scale = 1.0 / jnp.sum(powers, axis=1, keepdims=True)
            probs = (powers * scale).astype(BF16)
            part = jnp.dot(probs, v * half, preferred_element_type=F32)
            total = part if total is None else total + part
        ctx[tokens, c * SLAB + j * 128 : c * SLAB + (j + 1) * 128] = total.astype(BF16)

    def mix(b):
        tokens = slice(b * L, (b + 1) * L)
        mixed = jnp.concatenate(
            [
                jnp.dot(ctx[tokens, :], w_o[c, j], preferred_element_type=F32)
                for c in range(2)
                for j in range(3)
            ],
            axis=1,
        )
        values = x_ref[tokens, :].astype(F32) + mixed
        centered = values - jnp.mean(values, axis=1, keepdims=True)
        spread = jnp.mean(centered * centered, axis=1, keepdims=True)
        normed = centered * lax.rsqrt(spread + EPS) * gain_one_ref[...].reshape(
            1, D
        ) + shift_one_ref[...].reshape(1, D)
        normed = normed.astype(BF16)
        acc[tokens, :] = normed.astype(F32)
        first[tokens, :] = jnp.dot(normed, order, preferred_element_type=F32).astype(BF16)

    u_z.advance(2)
    project(0)
    send_rows_and_rotation()
    project(1)
    steps = {
        1: lambda: u_z.advance(3),
        3: o_x.done_x,
        5: share_e,
        6: share_rows,
        8: lambda: u_z.advance(4),
        11: lambda: d_y.advance(1),
    }
    for n, (c, p, j) in enumerate(
        (c, p, j) for c in range(2) for p in range(2) for j in range(3)
    ):
        attend(p, c, j)
        if n in steps:
            steps[n]()
    o_x.done()
    mix(0)
    mix(1)
    u_z.done()

    def raise_slabs(n, carry):
        for s in (2 * n, 2 * n + 1):
            for b in range(2):
                tokens = slice(b * L, (b + 1) * L)
                up = jnp.dot(first[tokens, :], w_u[s], preferred_element_type=F32)
                half = 0.5 * up
                act[s, tokens, :] = (half + half * lax.erf(up * (0.5**0.5))).astype(BF16)
        return carry

    def lower_slabs(n, carry):
        total = acc[...]
        for s in (2 * n, 2 * n + 1):
            total = total + lax.dot_general(
                act[s, :, 0:256], w_d[s], (((1,), (1,)), ((), ())), preferred_element_type=F32
            )
        last = jnp.concatenate([act[s, :, 256:SLAB] for s in (2 * n, 2 * n + 1)], axis=1)
        weights = jnp.concatenate([w_e[s] for s in (2 * n, 2 * n + 1)], axis=1)
        acc[...] = total + lax.dot_general(
            last, weights, (((1,), (1,)), ((), ())), preferred_element_type=F32
        )
        return carry

    lax.fori_loop(0, 4, raise_slabs, 0)
    d_y.advance(2)
    sems.arrived(w_e.at[pl.ds((1 - core) * 4, 4)], e_hand, sibling)
    d_y.done()
    lax.fori_loop(0, 4, lower_slabs, 0)

    token_at = lax.broadcasted_iota(jnp.int32, (L, 1), 0)
    for p in range(2):
        length = lens_ref[2 * tens + p]
        values = acc[p * L : (p + 1) * L, :]
        centered = values - jnp.mean(values, axis=1, keepdims=True)
        spread = jnp.mean(centered * centered, axis=1, keepdims=True)
        scaled = centered * lax.rsqrt(spread + EPS)
        pooled = jnp.sum(jnp.where(token_at < length, scaled, 0.0), axis=0, keepdims=True)
        emb = pooled / length.astype(F32) * gain_two_ref[...].reshape(1, D)
        emb_group[tens, p : p + 1, :] = emb + shift_two_ref[...].reshape(1, D)

    group_numbers = [sems.take() for _ in range(7)]
    for k in range(1, 8):
        sems.send(emb_group.at[tens], group_numbers[k - 1], peers[k - 1])
    sems.finish()
    for k in range(1, 8):
        origin = lax.rem(tens + 8 - k, 8)
        place = pl.ds(pl.multiple_of(origin * 96, 32), 96)
        sems.arrived(rot_out.at[place], rot_numbers[k - 1], peers[k - 1])
        sems.arrived(rows_out.at[origin], row_numbers[k - 1], peers[k - 1])
    for k in range(1, 8):
        other = lax.rem(tens + 8 - k, 8)
        sems.arrived(emb_group.at[other], group_numbers[k - 1], peers[k - 1])
    for t in range(8):
        both = emb_group[t]
        @pl.when(core == 0)
        def _():
            emb_out[0, y, z, 2 * t : 2 * t + 2, :] = both[:, :SLAB]
        @pl.when(core == 1)
        def _():
            emb_out[1, y, z, 2 * t : 2 * t + 2, :] = both[:, SLAB:]
    ze = Direct(sems, N_Z, z, at_z, lambda i: emb_out.at[core, y, i])

    def emb_parts(c, i):
        return emb_out.at[c, i, pl.ds(0, 4)], emb_out.at[c, i, pl.ds(4, 4)]

    ye = Spread(
        sems, N_Y, y, y_right, y_left, sibling,
        lambda i: emb_parts(core, i), lambda i: emb_parts(1 - core, i),
    )
    ze.begin()
    ze.done()
    ye.begin()
    ye.advance(1)
    ye.advance(2)
    ye.done()
    sems.finish()


def finish_kernel(emb_ref, ids_ref, rows_ref, rot_ref, weight_ref, old_ref, rotated_ref, centroids_ref, slot_ids, slots):
    step = pl.program_id(0)
    dp = lax.axis_index("dp")

    @pl.when(step == 0)
    def _():
        ids_row = jnp.transpose(ids_ref[...])[0:8, :]
        ids = ids_ref[pl.ds(pl.multiple_of(dp * 16, 16), 16), :]
        owners = jnp.floor(ids * (1.0 / 1024))
        owner_y = jnp.floor(owners * (1.0 / N_Z))
        owner_z = owners - owner_y * N_Z
        one = lax.broadcasted_iota(jnp.int32, (16, 16), 0)
        two = lax.broadcasted_iota(jnp.int32, (16, 16), 1)
        owners_row = jnp.sum(jnp.where(one == two, owners[:, 0:16], 0.0), axis=0, keepdims=True)
        rank = jnp.sum(
            ((owners[:, 0:16] == owners_row) & (two < one)).astype(F32), axis=1, keepdims=True
        )
        place = owner_z * 8.0 + rank * N_Y + owner_y
        spots = lax.broadcasted_iota(jnp.int32, (16, 64), 1).astype(F32)
        hot = (place[:, 0:64] == spots).astype(F32).astype(BF16)
        old = pick(hot, rows_ref[...])
        same = ids[:, 0:1] == ids_row[0:1, :]
        counts = jnp.sum(same.astype(F32), axis=1, keepdims=True)
        mine = jnp.floor(ids_row * (1.0 / 1024)) == dp.astype(F32)
        before = lax.broadcasted_iota(jnp.int32, (ROWS, ROWS), 0) < lax.broadcasted_iota(
            jnp.int32, (ROWS, ROWS), 1
        )
        spot = jnp.dot(
            mine.astype(F32).astype(BF16),
            before.astype(F32).astype(BF16),
            preferred_element_type=F32,
        )
        numbers = lax.broadcasted_iota(jnp.int32, (64, ROWS), 0).astype(F32)
        placed = (numbers == spot[0:1, :]) & mine[0:1, :]
        named = jnp.sum(jnp.where(placed, ids_row[0:1, :] + 1.0, 0.0), axis=1, keepdims=True)
        named = jnp.concatenate([named - 1.0, jnp.full((64, 1), -1.0, F32)], axis=0)
        slot_ids[...] = jnp.transpose(jnp.broadcast_to(named, (128, 128)))[0:8, :]
        taken = jnp.concatenate([same.astype(F32), placed.astype(F32)], axis=0).astype(BF16)
        weight = old[:, D : D + 1]
        result = None
        for h in range(2):
            picked = pick(taken, emb_ref[h])
            sums = picked[0:16, :]
            for k, part in enumerate(split3(picked[16:80, :])):
                slots[k * 64 : (k + 1) * 64, h * SLAB : (h + 1) * SLAB] = part
            centroids = (weight * old[:, h * SLAB : (h + 1) * SLAB] + sums) / (weight + counts)
            resid = emb_ref[h, pl.ds(pl.multiple_of(dp * 16, 16), 16), :] - centroids
            part = jnp.dot(
                resid,
                rot_ref[h * SLAB : (h + 1) * SLAB, :],
                precision=lax.Precision.HIGHEST,
                preferred_element_type=F32,
            )
            result = part if result is None else result + part
        rotated_ref[...] = result

    one = lax.broadcasted_iota(jnp.int32, (128, 128), 0)
    two = lax.broadcasted_iota(jnp.int32, (128, 128), 1)
    weight = jnp.concatenate(
        [
            jnp.sum(
                jnp.where(one == two, weight_ref[pl.ds(step * 4 + i, 1), :].astype(F32), 0.0),
                axis=1,
                keepdims=True,
            )
            for i in range(4)
        ],
        axis=0,
    )
    number = lax.broadcasted_iota(jnp.int32, (512, 64), 0) + dp * 1024 + step * 512
    hot = (number.astype(F32) == slot_ids[0:1, 0:64]).astype(F32)
    counts = jnp.sum(hot, axis=1, keepdims=True)
    hot = jnp.concatenate([hot, hot, hot], axis=1).astype(BF16)
    for h in range(2):
        columns = slice(h * SLAB, (h + 1) * SLAB)
        sums = jnp.dot(hot, slots[:, columns], preferred_element_type=F32)
        centroids_ref[:, columns] = (weight * old_ref[:, columns] + sums) / (weight + counts)


VMEM = pl.BlockSpec(memory_space=pltpu.VMEM)
HBM = pl.BlockSpec(memory_space=pltpu.HBM)


def local(
    hidden,
    lengths,
    owner_of,
    list_local,
    old_weight,
    old_centroids,
    w_qkv,
    w_out,
    gain_one,
    shift_one,
    w_up,
    w_down,
    gain_two,
    shift_two,
    rotation,
):
    vmem = pltpu.VMEM
    emb, ids, rows, rot = pl.pallas_call(
        encode_kernel,
        out_shape=(
            jax.ShapeDtypeStruct((2, N_Y, N_Z, 16, SLAB), F32),
            jax.ShapeDtypeStruct((N_Y, N_Z, 16, 128), F32),
            jax.ShapeDtypeStruct((8, 8, D + 128), F32),
            jax.ShapeDtypeStruct((D, 96), F32),
        ),
        in_specs=[HBM] * 15,
        out_specs=(VMEM,) * 4,
        scratch_shapes=[
            vmem((4, D, SLAB), BF16),
            vmem((8, D, SLAB), BF16),
            vmem((8, D, 256), BF16),
            vmem((8, D, 128), BF16),
            vmem((2, 3, D, 128), BF16),
            vmem((2, 3, D, 128), BF16),
            vmem((N_Z, 24, 2 * SLAB + 128), BF16),
            vmem((N_Y, 4, 24, SLAB), BF16),
            vmem((N_Z, 24, SLAB + 128), BF16),
            vmem((192, SLAB), F32),
            pltpu.SMEM((16,), jnp.int32),
            pltpu.SMEM((16,), jnp.int32),
            pltpu.SMEM((16,), jnp.int32),
            vmem((1024,), jnp.int32),
            vmem((D,), F32),
            vmem((D,), F32),
            vmem((D,), F32),
            vmem((D,), F32),
            vmem((ROWS, D), BF16),
            vmem((96, D), F32),
            vmem((1024, D), F32),
            vmem((8, 96, 96), F32),
            vmem((8, D + 128), F32),
            vmem((N_Y, 8, D + 128), F32),
            vmem((8, 2, D), F32),
            vmem((6, ROWS, SLAB), BF16),
            vmem((ROWS, D), BF16),
            vmem((ROWS, D), BF16),
            vmem((8, ROWS, SLAB), BF16),
            vmem((ROWS, D), F32),
            pltpu.SemaphoreType.DMA((N_COPIES,)),
            pltpu.SemaphoreType.DMA((N_COPIES,)),
            pltpu.SemaphoreType.DMA((17,)),
        ],
        compiler_params=pltpu.CompilerParams(
            collective_id=0, has_side_effects=True, vmem_limit_bytes=60 * 2**20
        ),
    )(
        lengths,
        owner_of.reshape(16),
        list_local,
        old_weight,
        gain_one,
        shift_one,
        gain_two,
        shift_two,
        hidden.reshape(ROWS, D),
        old_centroids,
        w_qkv,
        w_out,
        w_up,
        w_down.T,
        rotation,
    )
    whole = lambda *shape: pl.BlockSpec(shape, lambda i: (0,) * len(shape))
    return pl.pallas_call(
        finish_kernel,
        grid=(2,),
        out_shape=(
            jax.ShapeDtypeStruct((16, 96), F32),
            jax.ShapeDtypeStruct((1024, D), F32),
        ),
        in_specs=[
            whole(2, ROWS, SLAB),
            whole(ROWS, 128),
            whole(64, D + 128),
            whole(D, 96),
            whole(8, 128),
            pl.BlockSpec((512, D), lambda i: (i, 0)),
        ],
        out_specs=(whole(16, 96), pl.BlockSpec((512, D), lambda i: (i, 0))),
        scratch_shapes=[vmem((8, 128), F32), vmem((192, D), BF16)],
        compiler_params=pltpu.CompilerParams(vmem_limit_bytes=60 * 2**20),
    )(
        emb.reshape(2, ROWS, SLAB),
        ids.reshape(ROWS, 128),
        rows.reshape(64, D + 128),
        rot,
        old_weight.reshape(8, 128),
        old_centroids,
    )


def solution(mesh):
    return jax.shard_map(
        local,
        mesh=mesh,
        in_specs=(
            P(("dp", "tensor"), None, None),
            P("dp"),
            P("dp", None),
            P("dp"),
            P("dp"),
            P("dp", None),
            P("dp", None),
            P("dp", None),
            P(),
            P(),
            P("dp", "tensor"),
            P("tensor", "dp"),
            P(),
            P(),
            P("tensor", None),
        ),
        out_specs=(P("dp", "tensor"), P("dp", None)),
        check_vma=False,
    )
```
